256 devices in a mesh: dp: 32 (over y, z), expert: 8 (over x, core).
Axes of the slice: x: 4, y: 4, z: 8, core: 2. Of those that a mesh axis runs over, the one named last changes fastest.
Arguments:
- inputs: bfloat16 [32768, 2048], P(('dp', 'expert')), may hold values from -24 to 24
- grad_out: bfloat16 [32768, 2048], P(('dp', 'expert')), may hold values from -6 to 6
- expert_ids: int32 [32768, 2], P(('dp', 'expert')), may hold values from 0 to 7, all different within a row; in each aligned block of 128 rows (0 to 127, 128 to 255, ...) at most 64 rows name the same one
- gate_probs: bfloat16 [32768, 2], P(('dp', 'expert')), may hold values from 0.099609375 to 1
- w_gate: bfloat16 [8, 2048, 768], P('expert'), may hold values from -0.125 to 0.125
- w_up: bfloat16 [8, 2048, 768], P('expert'), may hold values from -0.125 to 0.125
- w_down: bfloat16 [8, 768, 2048], P('expert'), may hold values from -0.21875 to 0.21875
Outputs:
- grad_in: bfloat16 [32768, 2048], P(('dp', 'expert'))
- grad_gate: float32 [8, 2048, 768], P('expert', 'dp')
- grad_up: float32 [8, 2048, 768], P('expert', 'dp')
- grad_down: float32 [8, 768, 2048], P('expert', 'dp')
The draws below stay inside these ranges and needn't reach their ends.
Inputs may be any that keep to these rules, and one draw needn't show every extreme that they name: `expert_ids`: each row names 2 different experts; the 128 tokens of one device (aligned blocks of rows) name any one expert at most 64 times, a bound that some block reaches.
All inputs are finite; a program needn't handle non-finite values.
Results may differ from the reference program's by a relative error of at most 0.0065.
Values may be sent and summed in bfloat16 or wider, within the bound.
No kernel may reach another device: no remote copies, remote signals or barrier semaphores. Data moves between devices by JAX's collectives and lax.ppermute only.
A program may use at most 128 MiB of HBM per device.

```python
import math
import jax
import jax.numpy as jnp
import numpy as np
from jax import lax

D = 2048
FF = 768
TOPK = 2
TOK_DEV = 128
EXPERTS = 8
MOST = 64
GROUP = 1024
TOKENS = 32768
N_DP = 32
N_EXPERT = 8


def spiked(entries, stream_key, source, target, shards_of, factor):
    owner, partner = [(jnp.arange(entries.shape[axis_at]) // (entries.shape[axis_at] // shards_of)).reshape([-1 if axis == axis_at else 1 for axis in range(entries.ndim)]) for axis_at in (source, target)]
    chosen = jax.random.permutation(stream_key, shards_of)[partner]
    strong = (owner == chosen) | (owner == (partner + shards_of // 2) % shards_of)
    return jnp.where(strong, factor * entries, entries)


def steps_of(own_key, dims, cuts, least, largest):
    def one(position, blocks):
        heights = jax.random.uniform(jax.random.fold_in(jax.random.fold_in(own_key, 6), position), (blocks,), jnp.float32, least / len(cuts), largest / len(cuts))
        return jnp.repeat(jnp.exp(heights), dims[position] // blocks).reshape((-1,) + (1,) * (len(dims) - position - 1))

    gain = one(*cuts[0])
    for cut in cuts[1:]:
        gain = gain * one(*cut)
    return gain


def assign_block(rng, own, number, rows, amount, top, most, skew):
    order = jax.random.permutation(rng, amount)
    crowded, usual = portions_of(amount, rows * top, most, skew, True), portions_of(amount, rows * top, most, skew, False)
    places = jnp.arange(amount)

    def named(sizes, turn):
        used = int((sizes > 0).sum())
        fixed = max(1, used // 4)
        shifted = fixed + (places - fixed + turn * (used - fixed)) % max(1, amount - fixed)
        return jnp.zeros((amount,), jnp.int32).at[order[jnp.where(places < fixed, places, shifted)]].set(jnp.asarray(sizes, jnp.int32))

    sizes = jnp.where(number % 4 == 0, named(crowded, number // 4), named(usual, number - number // 4 - 1))
    mixed = jax.random.permutation(jax.random.fold_in(own, 3), amount)
    donor, taker = mixed[0:amount // 2 * 2:2], mixed[1:amount // 2 * 2:2]
    room = jnp.minimum(sizes[donor] - 1, most - sizes[taker]) // 2
    room = jnp.where((donor == order[0]) | (taker == order[0]) | (sizes[taker] == 0), 0, jnp.maximum(room, 0))
    shifted = jax.random.randint(jax.random.fold_in(own, 4), (amount // 2,), 0, 1 << 20) % (room + 1)
    sizes = sizes.at[donor].add(-shifted).at[taker].add(shifted)
    items = jnp.searchsorted(jnp.cumsum(sizes), jnp.arange(rows * top), side="right").astype(jnp.int32)
    grid = items.reshape(top, rows).T
    grid = grid[jax.random.permutation(jax.random.fold_in(own, 1), rows)]
    turn = jax.random.randint(jax.random.fold_in(own, 2), (rows, 1), 0, top)
    return jnp.take_along_axis(grid, (jnp.arange(top)[None, :] + turn) % top, axis=1)


def portions_of(count, total, bound, skew, full):
    portions = [(1 << 20) // math.isqrt(rank ** skew) + 1 for rank in range(1, count + 1)]
    largest = bound if full else min(bound, max(-(-total // count), total * portions[0] // sum(portions)))
    least = 1 if total - largest >= count - 1 else 0
    given, surplus = [largest] + [least] * (count - 1), total - largest - least * (count - 1)
    while surplus > 0:
        movable = [i for i in range(1, count) if given[i] < largest] or [i for i in range(1, count) if given[i] < bound]
        whole, left = sum([portions[i] for i in movable]), surplus
        for i in movable:
            extra = min(bound - given[i], max(1, left * portions[i] // whole), surplus)
            given[i] = given[i] + extra
            surplus = surplus - extra
    return np.array(given)


def centred(key, dims, spread, limit, split=(), held_as=jnp.bfloat16):
    values = spread * jax.random.normal(key, dims, jnp.float32)
    if split:
        values = values * steps_of(key, dims, split, -0.22, 0.18)
    return jnp.clip(values, -limit, limit).astype(held_as)


def noise_with(rng, dims, spread, reach, cuts, heavy, kind=jnp.bfloat16):
    result = spread * jax.random.normal(rng, dims, jnp.float32)
    if cuts:
        result = result * steps_of(rng, dims, cuts, -0.22, 0.18)
    return jnp.clip(spiked(result, jax.random.fold_in(rng, 3), *heavy), -reach, reach).astype(kind)


def setup_inputs(seed: int = 0) -> dict:
    splits = jax.random.split(jax.random.key(seed), 8)
    inputs = noise_with(splits[0], (TOKENS, D), 1.0, 24.0, ((0, 256),), (0, 1, 256, 6.0))
    grad_out = centred(splits[1], (TOKENS, D), 1.0, 6.0, ((0, 256),))
    expert_ids_keys = jax.random.split(jax.random.fold_in(splits[2], 1), TOKENS // TOK_DEV)
    expert_ids_turns = jax.random.permutation(jax.random.fold_in(splits[2], 3), TOKENS // TOK_DEV)
    expert_ids = jax.vmap(lambda own, number: assign_block(jax.random.fold_in(splits[2], 2), own, number, TOK_DEV, EXPERTS, TOPK, MOST, 2))(expert_ids_keys, expert_ids_turns).reshape((TOKENS, TOPK))
    gate_probs = jnp.clip(0.099609375 + 0.9003906 * jax.random.uniform(splits[3], (TOKENS, TOPK), jnp.float32) ** steps_of(splits[3], (TOKENS, TOPK), ((0, 256),), -0.2, 0.2), 0.099609375, 1.0).astype(jnp.bfloat16)
    w_gate = centred(splits[4], (EXPERTS, D, FF), D ** -0.5, 0.125, ((0, 8),))
    w_up = centred(splits[5], (EXPERTS, D, FF), D ** -0.5, 0.125, ((0, 8),))
    w_down = centred(splits[6], (EXPERTS, FF, D), FF ** -0.5, 0.21875, ((0, 8),))
    return {"inputs": inputs, "grad_out": grad_out, "expert_ids": expert_ids, "gate_probs": gate_probs, "w_gate": w_gate, "w_up": w_up, "w_down": w_down}


DIMS_ROWS = (((0,), (0,)), ((), ()))
DIMS_COLS = (((1,), (1,)), ((), ()))


def slot_table(routed, blocks, slot_most):
    per_block = routed.shape[0] // blocks
    shaped = routed.reshape(blocks, per_block)
    ranking = jnp.cumsum(shaped, axis=1, dtype=jnp.int32) - 1
    offsets = slot_most * jnp.arange(blocks, dtype=jnp.int32)[:, None]
    slot_ids = jnp.where(shaped > 0, ranking + offsets, blocks * slot_most).reshape(-1).astype(jnp.int32)
    source = jnp.arange(routed.shape[0], dtype=jnp.int32)
    slot_rows = jnp.zeros((blocks * slot_most,), jnp.int32).at[slot_ids].set(source, mode="drop")
    filled = jnp.zeros((blocks * slot_most,), jnp.float32).at[slot_ids].set(1.0, mode="drop")
    return slot_rows, filled


def expert_backward(rows_x, rows_grad, gate_w, up_w, down_w):
    pre_gate = jnp.dot(rows_x, gate_w, preferred_element_type=jnp.float32)
    pre_up = jnp.dot(rows_x, up_w, preferred_element_type=jnp.float32)
    sigmoid_gate = jax.nn.sigmoid(pre_gate)
    hidden = (pre_gate * sigmoid_gate * pre_up).astype(jnp.bfloat16)
    grad_hidden = lax.dot_general(rows_grad, down_w, DIMS_COLS, preferred_element_type=jnp.float32)
    grad_pre_gate = (grad_hidden * pre_up * sigmoid_gate * (1.0 + pre_gate * (1.0 - sigmoid_gate))).astype(jnp.bfloat16)
    grad_pre_up = (grad_hidden * pre_gate * sigmoid_gate).astype(jnp.bfloat16)
    input_term = (lax.dot_general(grad_pre_gate, gate_w, DIMS_COLS, preferred_element_type=jnp.float32)
                  + lax.dot_general(grad_pre_up, up_w, DIMS_COLS, preferred_element_type=jnp.float32)).astype(jnp.bfloat16)
    grad_gate = lax.dot_general(rows_x, grad_pre_gate, DIMS_ROWS, preferred_element_type=jnp.float32)
    grad_up = lax.dot_general(rows_x, grad_pre_up, DIMS_ROWS, preferred_element_type=jnp.float32)
    grad_down = lax.dot_general(hidden, rows_grad, DIMS_ROWS, preferred_element_type=jnp.float32)
    return input_term, grad_gate, grad_up, grad_down


def select_rows(batch_x, batch_grad, batch_ids, batch_gates, expert, blocks, slot_most):
    matches = batch_ids == expert
    routed = jnp.any(matches, axis=1).astype(jnp.int32)
    slot_rows, filled = slot_table(routed, blocks, slot_most)
    gate_rows = jnp.sum(jnp.where(matches, batch_gates.astype(jnp.float32), 0.0), axis=1)
    slot_gate = gate_rows[slot_rows] * filled
    rows_x = batch_x[slot_rows]
    rows_grad = (slot_gate[:, None] * batch_grad[slot_rows].astype(jnp.float32)).astype(jnp.bfloat16)
    return slot_rows, rows_x, rows_grad


def reference(inputs, grad_out, expert_ids, gate_probs, w_gate, w_up, w_down):
    def group_backward(carry, block):
        batch_x, batch_grad, batch_ids, batch_gates = block
        sum_gate, sum_up, sum_down = carry
        grad_sum = jnp.zeros((GROUP, D), jnp.float32)
        for expert in range(EXPERTS):
            slot_rows, rows_x, rows_grad = select_rows(batch_x, batch_grad, batch_ids, batch_gates, expert, N_EXPERT, MOST)
            input_term, grad_gate, grad_up, grad_down = expert_backward(rows_x, rows_grad, w_gate[expert], w_up[expert], w_down[expert])
            grad_sum = grad_sum.at[slot_rows].add(input_term.astype(jnp.float32))
            sum_gate = sum_gate.at[expert].add(grad_gate)
            sum_up = sum_up.at[expert].add(grad_up)
            sum_down = sum_down.at[expert].add(grad_down)
        return (sum_gate, sum_up, sum_down), grad_sum.astype(jnp.bfloat16)

    start = (jnp.zeros((EXPERTS, D, FF), jnp.float32), jnp.zeros((EXPERTS, D, FF), jnp.float32),
             jnp.zeros((EXPERTS, FF, D), jnp.float32))
    blocks_in = (inputs.reshape(N_DP, GROUP, D), grad_out.reshape(N_DP, GROUP, D),
                 expert_ids.reshape(N_DP, GROUP, TOPK), gate_probs.reshape(N_DP, GROUP, TOPK))
    totals, grad_batches = lax.scan(group_backward, start, blocks_in)
    return grad_batches.reshape(TOKENS, D), totals[0], totals[1], totals[2]
```

```python
import functools

import jax
import jax.numpy as jnp
from jax import lax
from jax.experimental import pallas as pl
from jax.experimental.pallas import tpu as pltpu
from jax.sharding import Mesh
from jax.sharding import PartitionSpec as P

BF = jnp.bfloat16
F32 = jnp.float32
ROWS = (((0,), (0,)), ((), ()))
COLS = (((1,), (1,)), ((), ()))
VMEM_LIMIT = 52 * 1024 * 1024


def shift(value, axis, step):
    n = lax.axis_size(axis)
    return lax.ppermute(value, axis, [(i, (i + step) % n) for i in range(n)])


def add(*terms):
    total = terms[0].astype(F32)
    for term in terms[1:]:
        total = total + term.astype(F32)
    return total.astype(BF)


def params():
    return pltpu.CompilerParams(vmem_limit_bytes=VMEM_LIMIT)


def one_hots(experts_ref, metas):
    own, partner = experts_ref[0].astype(F32), experts_ref[1].astype(F32)
    tables = [m[...].astype(F32) for m in metas]
    hits, gates = [], []
    for table in tables:
        first, second = table[0:1], table[1:2]
        for expert in (own, partner):
            hits.append(jnp.where((first == expert) | (second == expert), 1.0, 0.0))
            gates.append(
                jnp.where(first == expert, table[2:3], 0.0)
                + jnp.where(second == expert, table[3:4], 0.0)
            )
    hit = jnp.concatenate(hits, axis=0)
    tokens = hit.shape[1]
    before = lax.broadcasted_iota(jnp.int32, (tokens, tokens), 0)
    after = lax.broadcasted_iota(jnp.int32, (tokens, tokens), 1)
    upper = jnp.where(before <= after, 1.0, 0.0).astype(BF)
    rank = jnp.dot(hit.astype(BF), upper, preferred_element_type=F32)
    place = jnp.where(hit > 0.0, rank - 1.0, -1.0)
    slots = lax.broadcasted_iota(jnp.int32, (tokens // 2, tokens), 0).astype(F32)
    result = []
    for chip in range(len(tables)):
        halves, scale = [], []
        for k in (2 * chip, 2 * chip + 1):
            half = jnp.where(place[k : k + 1] == slots, 1.0, 0.0)
            halves.append(half)
            scale.append(jnp.sum(half * gates[k], axis=1, keepdims=True))
        result.append((jnp.concatenate(halves, axis=0).astype(BF), jnp.concatenate(scale, axis=0)))
    return result


def gather_kernel(scaled, experts_ref, *refs):
    metas, (a, b, c, d0, d1), (own_ref, partner_ref) = refs[:4], refs[4:9], refs[9:]
    blocks = [a[...], b[...], c[...], jnp.concatenate([d0[...], d1[...]], axis=0)]
    for k, (table, scale) in enumerate(one_hots(experts_ref, metas)):
        rows = jnp.dot(table, blocks[k], preferred_element_type=F32)
        if scaled:
            rows = scale * rows
        rows = rows.astype(BF)
        half = rows.shape[0] // 2
        own_ref[k * half : (k + 1) * half] = rows[:half]
        partner_ref[k * half : (k + 1) * half] = rows[half:]


def meta_specs(tokens):
    return [
        pl.BlockSpec((16, tokens), lambda i: (tokens // 16, 0)),
        pl.BlockSpec((16, tokens), lambda i: (tokens // 16, 0)),
        pl.BlockSpec((16, tokens), lambda i: (tokens // 16, 0)),
        pl.BlockSpec((16, tokens), lambda i: (tokens // 32, 0)),
    ]


def gather_rows(scaled, experts, metas, packets, tokens):
    width = packets[0].shape[1]
    tile = 512
    half = tokens // 2
    heights = (tokens, tokens, tokens, half, half)
    return pl.pallas_call(
        functools.partial(gather_kernel, scaled),
        grid=(width // tile,),
        in_specs=[pl.BlockSpec(memory_space=pltpu.SMEM)]
        + meta_specs(tokens)
        + [pl.BlockSpec((h, tile), lambda i: (0, i)) for h in heights],
        out_specs=[pl.BlockSpec((2 * tokens, tile), lambda i: (0, i))] * 2,
        out_shape=[jax.ShapeDtypeStruct((2 * tokens, width), BF)] * 2,
        compiler_params=params(),
        cost_estimate=pl.CostEstimate(
            flops=16 * tokens * tokens * width, bytes_accessed=16 * tokens * width, transcendentals=0
        ),
    )(experts, *metas, *packets)


def combine_kernel(experts_ref, *refs):
    metas, (own, partner), outs = refs[:4], refs[4:6], refs[6:]
    for k, (table, _) in enumerate(one_hots(experts_ref, metas)):
        half = table.shape[0] // 2
        part = slice(k * half, (k + 1) * half)
        terms = jnp.concatenate([own[part], partner[part]], axis=0)
        outs[k][...] = lax.dot_general(table, terms, ROWS, preferred_element_type=F32).astype(BF)


def combine(experts, metas, own, partner, tokens):
    width = own.shape[1]
    tile = 512
    return pl.pallas_call(
        combine_kernel,
        grid=(width // tile,),
        in_specs=[pl.BlockSpec(memory_space=pltpu.SMEM)]
        + meta_specs(tokens)
        + [pl.BlockSpec((2 * tokens, tile), lambda i: (0, i))] * 2,
        out_specs=[pl.BlockSpec((tokens, tile), lambda i: (0, i))] * 4,
        out_shape=[jax.ShapeDtypeStruct((tokens, width), BF)] * 4,
        compiler_params=params(),
        cost_estimate=pl.CostEstimate(
            flops=16 * tokens * tokens * width, bytes_accessed=16 * tokens * width, transcendentals=0
        ),
    )(experts, *metas, own, partner)


def forward_kernel(xa, xb, gate_w, up_w, hidden, to_gate, to_up):
    half = xa.shape[0]
    for k, x in enumerate((xa, xb)):
        rows = slice(k * half, (k + 1) * half)
        pre_gate = jnp.dot(x[...], gate_w[0], preferred_element_type=F32)
        pre_up = jnp.dot(x[...], up_w[0], preferred_element_type=F32)
        sigmoid = jax.nn.sigmoid(pre_gate)
        silu = pre_gate * sigmoid
        hidden[rows] = (silu * pre_up).astype(BF)
        to_gate[rows] = pre_up * sigmoid * (1.0 + pre_gate * (1.0 - sigmoid))
        to_up[rows] = silu


def forward(xa, xb, gate_w, up_w):
    half, width = xa.shape
    ff = gate_w.shape[2]
    tile = 256
    whole = pl.BlockSpec((half, width), lambda i: (0, 0))
    weight = pl.BlockSpec((1, width, tile), lambda i: (0, 0, i))
    out = pl.BlockSpec((2 * half, tile), lambda i: (0, i))
    return pl.pallas_call(
        forward_kernel,
        grid=(ff // tile,),
        in_specs=[whole, whole, weight, weight],
        out_specs=[out] * 3,
        out_shape=[
            jax.ShapeDtypeStruct((2 * half, ff), BF),
            jax.ShapeDtypeStruct((2 * half, ff), F32),
            jax.ShapeDtypeStruct((2 * half, ff), F32),
        ],
        compiler_params=params(),
        cost_estimate=pl.CostEstimate(
            flops=8 * half * width * ff, bytes_accessed=4 * width * ff + 24 * half * ff, transcendentals=2 * half * ff
        ),
    )(xa, xb, gate_w, up_w)


def weights_kernel(ny, nz, down_rows, gate_rows, *refs):
    xa, xb, ga, gb, hidden, to_gate, to_up, down_w, grad_gate, grad_up, part_a, part_b = refs
    step = pl.program_id(0)
    steps_down = ny // 2
    half = xa.shape[0]
    tile = down_w.shape[1]

    @pl.when(step < steps_down)
    def _():
        columns = pl.ds(pl.multiple_of(step * tile, 128), tile)
        grad = jnp.concatenate([ga[...], gb[...]], axis=0)
        grad_hidden = lax.dot_general(grad, down_w[0], COLS, preferred_element_type=F32)
        grad_gate[:, columns] = (grad_hidden * to_gate[...]).astype(BF)
        grad_up[:, columns] = (grad_hidden * to_up[...]).astype(BF)
        for c in range(grad.shape[1] // 256):
            block = lax.dot_general(
                hidden[...], grad[:, c * 256 : (c + 1) * 256], ROWS, preferred_element_type=F32
            )
            for y in range(2):
                for z in range(nz):
                    rows = block[(y * nz + z) * down_rows : (y * nz + z + 1) * down_rows]
                    rows = jnp.concatenate([rows[:, :128], rows[:, 128:]], axis=0).astype(BF)
                    part_b[z, 2 * step + y, c * 2 * down_rows : (c + 1) * 2 * down_rows] = rows

    @pl.when(step >= steps_down)
    def _():
        y = step - steps_down
        x = jnp.concatenate([xa[...], xb[...]], axis=0)
        for k, grad in enumerate((grad_gate, grad_up)):
            block = lax.dot_general(x, grad[...], ROWS, preferred_element_type=F32).astype(BF)
            blocks = grad.shape[1] // 128
            for z in range(nz):
                for c in range(blocks):
                    rows = block[z * gate_rows : (z + 1) * gate_rows, c * 128 : (c + 1) * 128]
                    at = (k * blocks + c) * gate_rows
                    if at < part_a.shape[2]:
                        part_a[0, z, at : at + gate_rows] = rows
                    else:
                        at = at - part_a.shape[2] + blocks * gate_rows
                        part_b[z, y, at : at + gate_rows] = rows


def weight_grads(xa, xb, ga, gb, hidden, to_gate, to_up, down_w, ny, nz):
    half, width = xa.shape
    ff = hidden.shape[1]
    down_rows, gate_rows = ff // (ny * nz), width // (ny * nz)
    lines = 3 * gate_rows * ff // 128
    lines_a = lines // 2
    down = ny // 2
    tile = ff // down
    first = lambda i: jnp.minimum(i, down - 1)
    later = lambda i: jnp.maximum(i - down, 0)
    once = pl.Buffered(1)
    x_spec = pl.BlockSpec((half, width // ny), lambda i: (0, later(i)))
    g_spec = pl.BlockSpec((half, width), lambda i: (0, 0))
    f_spec = pl.BlockSpec((2 * half, tile), lambda i: (0, first(i)))
    grad_spec = pl.BlockSpec((2 * half, ff), lambda i: (0, 0))
    return pl.pallas_call(
        functools.partial(weights_kernel, ny, nz, down_rows, gate_rows),
        grid=(down + ny,),
        in_specs=[
            x_spec,
            x_spec,
            g_spec,
            g_spec,
            f_spec,
            f_spec,
            f_spec,
            pl.BlockSpec((1, tile, width), lambda i: (0, first(i), 0)),
        ],
        out_specs=[
            grad_spec,
            grad_spec,
            pl.BlockSpec((1, nz, lines_a, 128), lambda i: (later(i), 0, 0, 0)),
            pl.BlockSpec((nz, ny, lines - lines_a, 128), lambda i: (0, 0, 0, 0)),
        ],
        out_shape=[
            jax.ShapeDtypeStruct((2 * half, ff), BF),
            jax.ShapeDtypeStruct((2 * half, ff), BF),
            jax.ShapeDtypeStruct((ny, nz, lines_a, 128), BF),
            jax.ShapeDtypeStruct((nz, ny, lines - lines_a, 128), BF),
        ],
        compiler_params=params(),
        cost_estimate=pl.CostEstimate(
            flops=16 * half * width * ff, bytes_accessed=8 * width * ff + 8 * half * width, transcendentals=0
        ),
    )(xa, xb, ga, gb, hidden, to_gate, to_up, down_w)


def terms_kernel(grad_gate, grad_up, gate_w, up_w, first, second):
    half = first.shape[0]
    total = lax.dot_general(grad_gate[...], gate_w[0], COLS, preferred_element_type=F32)
    total = total + lax.dot_general(grad_up[...], up_w[0], COLS, preferred_element_type=F32)
    total = total.astype(BF)
    first[...] = total[:half]
    second[...] = total[half:]


def input_terms(grad_gate, grad_up, gate_w, up_w):
    slots, ff = grad_gate.shape
    width = gate_w.shape[1]
    tile = 512
    grad = pl.BlockSpec((slots, ff), lambda i: (0, 0))
    weight = pl.BlockSpec((1, tile, ff), lambda i: (0, i, 0))
    out = pl.BlockSpec((slots // 2, tile), lambda i: (0, i))
    return pl.pallas_call(
        terms_kernel,
        grid=(width // tile,),
        in_specs=[grad, grad, weight, weight],
        out_specs=[out, out],
        out_shape=[jax.ShapeDtypeStruct((slots // 2, width), BF)] * 2,
        compiler_params=params(),
        cost_estimate=pl.CostEstimate(
            flops=4 * slots * width * ff, bytes_accessed=4 * width * ff + 2 * slots * width, transcendentals=0
        ),
    )(grad_gate, grad_up, gate_w, up_w)


def ring_sum(value, axis):
    n = value.shape[0]
    me = lax.axis_index(axis)
    half = value.shape[1] // 2
    chunk = lambda k: lax.dynamic_index_in_dim(value, (me + k + n) % n, 0, keepdims=False)
    low = lambda k: chunk(k)[:half]
    high = lambda k: chunk(k)[half:]
    far = n // 2
    right = jnp.concatenate([low(far), high(far - 1)], axis=0)
    left = jnp.concatenate([low(1 - far), high(far)], axis=0)
    for k in range(far - 1, 1, -1):
        from_left, from_right = shift(right, axis, 1), shift(left, axis, -1)
        right = add(jnp.concatenate([low(k), high(k - 1)], axis=0), from_left)
        left = add(jnp.concatenate([low(1 - k), high(-k)], axis=0), from_right)
    from_left, from_right = shift(right, axis, 1), shift(left, axis, -1)
    right = add(low(1), from_left[:half])
    left = add(high(-1), from_right[half:])
    last_left, last_right = shift(right, axis, 1), shift(left, axis, -1)
    return (
        chunk(0).astype(F32)
        + jnp.concatenate([from_right[:half], from_left[half:]], axis=0).astype(F32)
        + jnp.concatenate([last_left, last_right], axis=0).astype(F32)
    )


def shards(inputs, grad_out, expert_ids, gate_probs, w_gate, w_up, w_down):
    tokens, width = inputs.shape
    ff = w_gate.shape[2]
    ny, nz = lax.axis_size("y"), lax.axis_size("z")
    half = tokens // 2
    chip, core = lax.axis_index("x"), lax.axis_index("core")
    experts = jnp.stack([2 * chip + core, 2 * chip + 1 - core]).astype(jnp.int32)

    table = jnp.concatenate([expert_ids.T.astype(BF), gate_probs.T], axis=0)
    table = jnp.pad(table, ((0, 12), (0, width - tokens)))
    packet = jnp.concatenate([inputs, table], axis=0)

    x_left, x_right = shift(packet, "x", 1), shift(packet, "x", -1)
    g_left, g_right = shift(grad_out, "x", 1), shift(grad_out, "x", -1)
    x_low, x_high = shift(x_left[:half], "x", 1), shift(x_right[half:], "x", -1)
    g_low, g_high = shift(g_left[:half], "x", 1), shift(g_right[half:], "x", -1)
    metas = (packet, x_left, x_right, x_high)

    xa, x_partner = gather_rows(False, experts, metas, (packet, x_left, x_right, x_low, x_high), tokens)
    xb = shift(x_partner, "core", 1)
    hidden, to_gate, to_up = forward(xa, xb, w_gate, w_up)
    ga, g_partner = gather_rows(True, experts, metas, (grad_out, g_left, g_right, g_low, g_high), tokens)
    gb = shift(g_partner, "core", 1)
    grad_gate, grad_up, part_a, part_b = weight_grads(
        xa, xb, ga, gb, hidden, to_gate, to_up, w_down, ny, nz
    )

    sum_a = ring_sum(part_a, "y").astype(BF)
    sum_b = ring_sum(part_b, "z").astype(BF)
    sum_a = ring_sum(sum_a, "z")
    sum_b = ring_sum(sum_b, "y")

    term_own, term_other = input_terms(grad_gate, grad_up, w_gate, w_up)
    term_partner = shift(term_other, "core", 1)
    mine, for_left, for_right, for_far = combine(experts, metas, term_own, term_partner, tokens)
    back = (shift(for_left, "x", -1), shift(for_right, "x", 1), shift(for_far, "x", 2))
    grad_in = add(mine, *back)

    gate_rows, down_rows = width // (ny * nz), ff // (ny * nz)
    lines = gate_rows * ff // 128
    columns = lambda v: v.reshape(-1, gate_rows, 128).transpose(1, 0, 2).reshape(gate_rows, -1)
    out_gate = columns(sum_a[:lines])
    out_up = jnp.concatenate([columns(sum_a[lines:]), columns(sum_b[lines:])], axis=1)
    out_down = sum_b[:lines].reshape(-1, down_rows, 128).transpose(1, 0, 2).reshape(down_rows, width)
    return grad_in, out_gate[None], out_up[None], out_down[None]


def solution(mesh):
    fine = Mesh(mesh.devices.reshape(4, 8, 4, 2), ("y", "z", "x", "core"))
    row = P(("y", "z", "x", "core"), None)
    weight = P(("x", "core"), None, None)
    summed = P(("x", "core"), ("y", "z"), None)
    return jax.shard_map(
        shards,
        mesh=fine,
        in_specs=(row, row, row, row, weight, weight, weight),
        out_specs=(row, summed, summed, summed),
        check_vma=False,
    )
```

```python
import functools

import jax
import jax.numpy as jnp
from jax import lax
from jax.experimental import pallas as pl
from jax.experimental.pallas import tpu as pltpu
from jax.sharding import Mesh
from jax.sharding import PartitionSpec as P

BF = jnp.bfloat16
F32 = jnp.float32
ROWS = (((0,), (0,)), ((), ()))
COLS = (((1,), (1,)), ((), ()))
VMEM_LIMIT = 36 * 1024 * 1024


def shift(value, axis, step):
    n = lax.axis_size(axis)
    return lax.ppermute(value, axis, [(i, (i + step) % n) for i in range(n)])


def add(*terms):
    total = terms[0].astype(F32)
    for term in terms[1:]:
        total = total + term.astype(F32)
    return total.astype(BF)


def params():
    return pltpu.CompilerParams(vmem_limit_bytes=VMEM_LIMIT)


def one_hots(experts_ref, metas):
    own, partner = experts_ref[0].astype(F32), experts_ref[1].astype(F32)
    tables = [m[...].astype(F32) for m in metas]
    hits, gates = [], []
    for table in tables:
        first, second = table[0:1], table[1:2]
        for expert in (own, partner):
            hits.append(jnp.where((first == expert) | (second == expert), 1.0, 0.0))
            gates.append(
                jnp.where(first == expert, table[2:3], 0.0)
                + jnp.where(second == expert, table[3:4], 0.0)
            )
    hit = jnp.concatenate(hits, axis=0)
    tokens = hit.shape[1]
    before = lax.broadcasted_iota(jnp.int32, (tokens, tokens), 0)
    after = lax.broadcasted_iota(jnp.int32, (tokens, tokens), 1)
    upper = jnp.where(before <= after, 1.0, 0.0).astype(BF)
    rank = jnp.dot(hit.astype(BF), upper, preferred_element_type=F32)
    place = jnp.where(hit > 0.0, rank - 1.0, -1.0)
    slots = lax.broadcasted_iota(jnp.int32, (tokens // 2, tokens), 0).astype(F32)
    result = []
    for chip in range(len(tables)):
        halves, scale = [], []
        for k in (2 * chip, 2 * chip + 1):
            half = jnp.where(place[k : k + 1] == slots, 1.0, 0.0)
            halves.append(half)
            scale.append(jnp.sum(half * gates[k], axis=1, keepdims=True))
        result.append((jnp.concatenate(halves, axis=0).astype(BF), jnp.concatenate(scale, axis=0)))
    return result


def fill_tables(experts_ref, metas, table_ref, scale_ref):
    @pl.when(pl.program_id(0) == 0)
    def _():
        for k, (table, scale) in enumerate(one_hots(experts_ref, metas)):
            table_ref[k] = table
            scale_ref[k] = jnp.broadcast_to(scale, scale_ref.shape[1:])


def table_scratch(tokens):
    return [pltpu.VMEM((4, tokens, tokens), BF), pltpu.VMEM((4, tokens, 128), F32)]


def gather_kernel(scaled, experts_ref, *refs):
    metas, (a, b, c, d0, d1), (own_ref, partner_ref) = refs[:4], refs[4:9], refs[9:11]
    table_ref, scale_ref = refs[11:]
    fill_tables(experts_ref, metas, table_ref, scale_ref)
    blocks = [a[...], b[...], c[...], jnp.concatenate([d0[...], d1[...]], axis=0)]
    for k in range(4):
        rows = jnp.dot(table_ref[k], blocks[k], preferred_element_type=F32)
        if scaled:
            rows = scale_ref[k][:, :1] * rows
        rows = rows.astype(BF)
        half = rows.shape[0] // 2
        own_ref[k * half : (k + 1) * half] = rows[:half]
        partner_ref[k * half : (k + 1) * half] = rows[half:]


def meta_specs(tokens):
    return [
        pl.BlockSpec((16, tokens), lambda i: (tokens // 16, 0)),
        pl.BlockSpec((16, tokens), lambda i: (tokens // 16, 0)),
        pl.BlockSpec((16, tokens), lambda i: (tokens // 16, 0)),
        pl.BlockSpec((16, tokens), lambda i: (tokens // 32, 0)),
    ]


def gather_rows(scaled, experts, metas, packets, tokens):
    width = packets[0].shape[1]
    tile = 512
    half = tokens // 2
    heights = (tokens, tokens, tokens, half, half)
    return pl.pallas_call(
        functools.partial(gather_kernel, scaled),
        grid=(width // tile,),
        in_specs=[pl.BlockSpec(memory_space=pltpu.SMEM)]
        + meta_specs(tokens)
        + [pl.BlockSpec((h, tile), lambda i: (0, i)) for h in heights],
        out_specs=[pl.BlockSpec((2 * tokens, tile), lambda i: (0, i))] * 2,
        out_shape=[jax.ShapeDtypeStruct((2 * tokens, width), BF)] * 2,
        scratch_shapes=table_scratch(tokens),
        compiler_params=params(),
        cost_estimate=pl.CostEstimate(
            flops=16 * tokens * tokens * width, bytes_accessed=16 * tokens * width, transcendentals=0
        ),
    )(experts, *metas, *packets)


def combine_kernel(experts_ref, *refs):
    metas, (own, partner), outs = refs[:4], refs[4:6], refs[6:10]
    table_ref, scale_ref = refs[10:]
    fill_tables(experts_ref, metas, table_ref, scale_ref)
    for k in range(4):
        table = table_ref[k]
        half = table.shape[0] // 2
        part = slice(k * half, (k + 1) * half)
        terms = jnp.concatenate([own[part], partner[part]], axis=0)
        outs[k][...] = lax.dot_general(table, terms, ROWS, preferred_element_type=F32).astype(BF)


def combine(experts, metas, own, partner, tokens):
    width = own.shape[1]
    tile = 512
    return pl.pallas_call(
        combine_kernel,
        grid=(width // tile,),
        in_specs=[pl.BlockSpec(memory_space=pltpu.SMEM)]
        + meta_specs(tokens)
        + [pl.BlockSpec((2 * tokens, tile), lambda i: (0, i))] * 2,
        out_specs=[pl.BlockSpec((tokens, tile), lambda i: (0, i))] * 4,
        out_shape=[jax.ShapeDtypeStruct((tokens, width), BF)] * 4,
        scratch_shapes=table_scratch(tokens),
        compiler_params=params(),
        cost_estimate=pl.CostEstimate(
            flops=tokens * width, bytes_accessed=tokens * width, transcendentals=0
        ),
    )(experts, *metas, own, partner)


def forward_kernel(xa, xb, gate_w, up_w, hidden, to_gate, to_up):
    half = xa.shape[0]
    for k, x in enumerate((xa, xb)):
        rows = slice(k * half, (k + 1) * half)
        pre_gate = jnp.dot(x[...], gate_w[0], preferred_element_type=F32)
        pre_up = jnp.dot(x[...], up_w[0], preferred_element_type=F32)
        sigmoid = jax.nn.sigmoid(pre_gate)
        silu = pre_gate * sigmoid
        hidden[rows] = (silu * pre_up).astype(BF)
        to_gate[rows] = pre_up * sigmoid * (1.0 + pre_gate * (1.0 - sigmoid))
        to_up[rows] = silu


def forward(xa, xb, gate_w, up_w):
    half, width = xa.shape
    ff = gate_w.shape[2]
    tile = 256
    whole = pl.BlockSpec((half, width), lambda i: (0, 0))
    weight = pl.BlockSpec((1, width, tile), lambda i: (0, 0, i))
    out = pl.BlockSpec((2 * half, tile), lambda i: (0, i))
    return pl.pallas_call(
        forward_kernel,
        grid=(ff // tile,),
        in_specs=[whole, whole, weight, weight],
        out_specs=[out] * 3,
        out_shape=[
            jax.ShapeDtypeStruct((2 * half, ff), BF),
            jax.ShapeDtypeStruct((2 * half, ff), F32),
            jax.ShapeDtypeStruct((2 * half, ff), F32),
        ],
        compiler_params=params(),
        cost_estimate=pl.CostEstimate(
            flops=8 * half * width * ff, bytes_accessed=4 * width * ff + 24 * half * ff, transcendentals=2 * half * ff
        ),
    )(xa, xb, gate_w, up_w)


def down_kernel(ny, nz, down_rows, gate_rows, me_ref, *refs):
    xa, xb, ga, gb, hidden, to_gate, to_up, down_w, grad_gate, grad_up, part, right, left = refs
    step = pl.program_id(0)
    steps_down = ny // 2
    tile = down_w.shape[1]
    width = xa.shape[1]
    rel = lambda z: lax.rem(z - me_ref[1] + nz, nz)

    @pl.when(step < steps_down)
    def _():
        columns = pl.ds(pl.multiple_of(step * tile, 128), tile)
        grad = jnp.concatenate([ga[...], gb[...]], axis=0)
        grad_hidden = lax.dot_general(grad, down_w[0], COLS, preferred_element_type=F32)
        grad_gate[:, columns] = (grad_hidden * to_gate[...]).astype(BF)
        grad_up[:, columns] = (grad_hidden * to_up[...]).astype(BF)
        block = lax.dot_general(hidden[...], grad, ROWS, preferred_element_type=F32)
        for y in range(2):
            for z in range(nz):
                rows = block[(y * nz + z) * down_rows : (y * nz + z + 1) * down_rows]
                for c in range(width // 256):
                    pair = [rows[:, c * 256 : c * 256 + 128], rows[:, c * 256 + 128 : c * 256 + 256]]
                    pair = jnp.concatenate(pair, axis=0).astype(BF)
                    part[rel(z), 2 * step + y, c * 2 * down_rows : (c + 1) * 2 * down_rows] = pair

    @pl.when(step == steps_down)
    def _():
        half = grad_up.shape[1] // 2
        lines = down_rows * width // 128
        deep = width // ny
        for y in range(ny):
            x = jnp.concatenate(
                [xa[:, y * deep : (y + 1) * deep], xb[:, y * deep : (y + 1) * deep]], axis=0
            )
            block = lax.dot_general(x, grad_up[:, half:], ROWS, preferred_element_type=F32)
            for z in range(nz):
                for c in range(half // 128):
                    rows = block[z * gate_rows : (z + 1) * gate_rows, c * 128 : (c + 1) * 128]
                    at = lines + c * gate_rows
                    part[rel(z), y, at : at + gate_rows] = rows.astype(BF)
        near, far, h = nz // 2 - 1, nz // 2, ny // 2
        right[:h], right[h:] = part[far, :h], part[near, h:]
        left[:h], left[h:] = part[nz - near, :h], part[far, h:]


def down_grads(me, xa, xb, ga, gb, hidden, to_gate, to_up, down_w, ny, nz):
    half, width = xa.shape
    ff = hidden.shape[1]
    down_rows, gate_rows = ff // (ny * nz), width // (ny * nz)
    lines = 3 * gate_rows * ff // 256
    down = ny // 2
    tile = ff // down
    first = lambda i: jnp.minimum(i, down - 1)
    g_spec = pl.BlockSpec((half, width), lambda i, m: (0, 0))
    f_spec = pl.BlockSpec((2 * half, tile), lambda i, m: (0, first(i)))
    grad_spec = pl.BlockSpec((2 * half, ff), lambda i, m: (0, 0))
    sent = pl.BlockSpec((ny, lines, 128), lambda i, m: (0, 0, 0))
    return pl.pallas_call(
        functools.partial(down_kernel, ny, nz, down_rows, gate_rows),
        grid_spec=pltpu.PrefetchScalarGridSpec(
            num_scalar_prefetch=1,
            grid=(down + 1,),
            in_specs=[g_spec] * 4
            + [f_spec] * 3
            + [pl.BlockSpec((1, tile, width), lambda i, m: (0, first(i), 0))],
            out_specs=[
                grad_spec,
                grad_spec,
                pl.BlockSpec((nz, ny, lines, 128), lambda i, m: (0, 0, 0, 0)),
                sent,
                sent,
            ],
        ),
        out_shape=[
            jax.ShapeDtypeStruct((2 * half, ff), BF),
            jax.ShapeDtypeStruct((2 * half, ff), BF),
            jax.ShapeDtypeStruct((nz, ny, lines, 128), BF),
            jax.ShapeDtypeStruct((ny, lines, 128), BF),
            jax.ShapeDtypeStruct((ny, lines, 128), BF),
        ],
        compiler_params=params(),
        cost_estimate=pl.CostEstimate(
            flops=10 * half * width * ff, bytes_accessed=4 * width * ff + 8 * half * width, transcendentals=0
        ),
    )(me, xa, xb, ga, gb, hidden, to_gate, to_up, down_w)


def gate_kernel(nz, gate_rows, me_ref, xa, xb, grad_gate, grad_up, *refs):
    outs, grads = refs[:-1], refs[-1]
    ff = grad_gate.shape[1]

    @pl.when(pl.program_id(0) == 0)
    def _():
        grads[:, :ff] = grad_gate[...]
        grads[:, ff:] = grad_up[:, : ff // 2]

    x = jnp.concatenate([xa[...], xb[...]], axis=0)
    block = lax.dot_general(x, grads[...], ROWS, preferred_element_type=F32)
    each = nz // len(outs)
    for z in range(nz):
        for c in range(grads.shape[1] // 128):
            rows = block[z * gate_rows : (z + 1) * gate_rows, c * 128 : (c + 1) * 128]
            outs[z // each][0, z % each, c * gate_rows : (c + 1) * gate_rows] = rows.astype(BF)


def gate_grads(me, xa, xb, grad_gate, grad_up, ny, nz, far):
    half, width = xa.shape
    ff = grad_gate.shape[1]
    gate_rows = width // (ny * nz)
    lines = 3 * gate_rows * ff // 256
    steps = 1 if far else 3
    turn = lambda i: 2 if far else jnp.where(i == 0, 1, jnp.where(i == 1, 3, 0))
    place = lambda i: 0 if far else jnp.minimum(turn(i), 2)
    x_spec = pl.BlockSpec((half, width // ny), lambda i, m: (0, lax.rem(m[0] + turn(i), ny)))
    grad_spec = pl.BlockSpec((2 * half, ff), lambda i, m: (0, 0))
    outs = 2 if far else 1
    return pl.pallas_call(
        functools.partial(gate_kernel, nz, gate_rows),
        grid_spec=pltpu.PrefetchScalarGridSpec(
            num_scalar_prefetch=1,
            grid=(steps,),
            in_specs=[x_spec, x_spec, grad_spec, grad_spec],
            out_specs=[pl.BlockSpec((1, nz // outs, lines, 128), lambda i, m: (place(i), 0, 0, 0))] * outs,
            scratch_shapes=[pltpu.VMEM((2 * half, ff + ff // 2), BF)],
        ),
        out_shape=[jax.ShapeDtypeStruct((steps, nz // outs, lines, 128), BF)] * outs,
        compiler_params=params(),
        cost_estimate=pl.CostEstimate(
            flops=2 * steps * half * width * ff, bytes_accessed=steps * (half * width + width * ff), transcendentals=0
        ),
    )(me, xa, xb, grad_gate, grad_up)


def terms_kernel(grad_gate, grad_up, gate_w, up_w, first, second):
    half = first.shape[0]
    total = lax.dot_general(grad_gate[...], gate_w[0], COLS, preferred_element_type=F32)
    total = total + lax.dot_general(grad_up[...], up_w[0], COLS, preferred_element_type=F32)
    total = total.astype(BF)
    first[...] = total[:half]
    second[...] = total[half:]


def input_terms(grad_gate, grad_up, gate_w, up_w):
    slots, ff = grad_gate.shape
    width = gate_w.shape[1]
    tile = 512
    grad = pl.BlockSpec((slots, ff), lambda i: (0, 0))
    weight = pl.BlockSpec((1, tile, ff), lambda i: (0, i, 0))
    out = pl.BlockSpec((slots // 2, tile), lambda i: (0, i))
    return pl.pallas_call(
        terms_kernel,
        grid=(width // tile,),
        in_specs=[grad, grad, weight, weight],
        out_specs=[out, out],
        out_shape=[jax.ShapeDtypeStruct((slots // 2, width), BF)] * 2,
        compiler_params=params(),
        cost_estimate=pl.CostEstimate(
            flops=slots * ff, bytes_accessed=slots * ff, transcendentals=0
        ),
    )(grad_gate, grad_up, gate_w, up_w)


def cat(first, second):
    return jnp.concatenate([first, second], axis=0)


class Blocks:
    def __init__(self, value, axis, counted_from_here):
        self.value, self.axis, self.n = value, axis, lax.axis_size(axis)
        self.half = value.shape[1] // 2
        self.start = 0 if counted_from_here else lax.axis_index(axis)

    def block(self, k):
        if self.value.shape[0] == self.n - 1:
            return self.value[min(k % self.n, self.n - 2)]
        return lax.dynamic_index_in_dim(self.value, (self.start + k + self.n) % self.n, 0, keepdims=False)

    def low(self, k):
        return self.block(k)[: self.half]

    def high(self, k):
        return self.block(k)[self.half :]

    def send(self, right, left):
        return shift(right, self.axis, 1), shift(left, self.axis, -1)

    def total(self, *pairs):
        result = self.block(0).astype(F32)
        for low, high in pairs:
            result = result + cat(low, high).astype(F32)
        return result


def shards(inputs, grad_out, expert_ids, gate_probs, w_gate, w_up, w_down):
    tokens, width = inputs.shape
    ff = w_gate.shape[2]
    ny, nz = lax.axis_size("y"), lax.axis_size("z")
    half = tokens // 2
    chip, core = lax.axis_index("x"), lax.axis_index("core")
    experts = jnp.stack([2 * chip + core, 2 * chip + 1 - core]).astype(jnp.int32)
    me = jnp.stack([lax.axis_index("y"), lax.axis_index("z")]).astype(jnp.int32)
    fence = lax.optimization_barrier

    table = jnp.concatenate([expert_ids.T.astype(BF), gate_probs.T], axis=0)
    table = jnp.pad(table, ((0, 12), (0, width - tokens)))
    packet = jnp.concatenate([inputs, table], axis=0)

    x_left, x_right = shift(packet, "x", 1), shift(packet, "x", -1)
    x_left, x_right, later = fence((x_left, x_right, grad_out))
    g_left, g_right = shift(later, "x", 1), shift(later, "x", -1)
    x_low, x_high = shift(x_left[:half], "x", 1), shift(x_right[half:], "x", -1)
    g_low, g_high = shift(g_left[:half], "x", 1), shift(g_right[half:], "x", -1)
    metas = (packet, x_left, x_right, x_high)

    xa, x_partner = gather_rows(False, experts, metas, (packet, x_left, x_right, x_low, x_high), tokens)
    xb = shift(x_partner, "core", 1)
    hidden, to_gate, to_up = forward(xa, xb, w_gate, w_up)
    ga, g_partner = gather_rows(True, experts, metas, (grad_out, g_left, g_right, g_low, g_high), tokens)
    gb = shift(g_partner, "core", 1)
    grad_gate, grad_up, part_b, b_right, b_left = down_grads(
        me, xa, xb, ga, gb, hidden, to_gate, to_up, w_down, ny, nz
    )

    b = Blocks(part_b, "z", True)
    h = b.half
    z1 = b.send(b_right, b_left)
    a_low, a_high = gate_grads(me, xa, xb, grad_gate, grad_up, ny, nz, True)
    a_low, a_high, grads = fence((a_low[0], a_high[0], (grad_gate, grad_up)))
    y1 = shift(a_low, "y", 1), shift(a_high, "y", -1)
    (part_a,) = gate_grads(me, xa, xb, *grads, ny, nz, False)
    part_a, grads = fence((part_a, grads))
    a = Blocks(part_a, "y", True)
    terms = input_terms(*grads, w_gate, w_up)

    ops = (add(cat(b.low(3), b.high(2)), z1[0]), add(cat(b.low(-2), b.high(-3)), z1[1]))
    ops, (term_own, term_other) = fence((ops, terms))
    z2 = b.send(*ops)
    term_partner = shift(term_other, "core", 1)

    ops, y1 = fence(((a.high(1), a.low(-1)), y1))
    y2 = a.send(*ops)

    ops = (add(cat(b.low(2), b.high(1)), z2[0]), add(cat(b.low(-1), b.high(-2)), z2[1]))
    ops, (term_own, term_partner) = fence((ops, (term_own, term_partner)))
    z3 = b.send(*ops)
    blocks = combine(experts, metas, term_own, term_partner, tokens)

    ops, y2 = fence(((add(a.low(1), y1[0]), add(a.high(-1), y1[1])), y2))
    y3 = a.send(*ops)

    ops = (add(b.low(1), z3[0][:h]), add(b.high(-1), z3[1][h:]))
    z4 = b.send(*fence(ops))

    a = Blocks(a.total((y2[1], y2[0]), y3).astype(BF), "z", False)
    u = a.half
    ops = (cat(a.low(4), a.high(3)), cat(a.low(-3), a.high(4)))
    ops, (mine, for_left, for_right, for_far) = fence((ops, blocks))
    z5 = a.send(*ops)
    from_far = shift(for_far, "x", 2)

    b = Blocks(b.total((z3[1][:h], z3[0][h:]), z4).astype(BF), "y", False)
    ops = (cat(b.low(2), b.high(1)), cat(b.low(-1), b.high(2)))
    ops, from_far, for_left = fence((ops, from_far, for_left))
    y4 = b.send(*ops)
    from_right = shift(for_left, "x", -1)

    ops = (add(cat(a.low(3), a.high(2)), z5[0]), add(cat(a.low(-2), a.high(-3)), z5[1]))
    z6 = a.send(*fence(ops))

    y5 = b.send(*fence((add(b.low(1), y4[0][:u]), add(b.high(-1), y4[1][u:]))))
    ops = (add(cat(a.low(2), a.high(1)), z6[0]), add(cat(a.low(-1), a.high(-2)), z6[1]))
    ops, from_right, for_right = fence((ops, from_right, for_right))
    z7 = a.send(*ops)
    from_left = shift(for_right, "x", 1)
    ops, y5 = fence(((add(a.low(1), z7[0][:u]), add(a.high(-1), z7[1][u:])), y5))
    z8 = a.send(*ops)
    grad_in = add(mine, from_far, from_right, from_left)
    sum_b = b.total((y4[1][:u], y4[0][u:]), y5)
    sum_a = a.total((z7[1][:u], z7[0][u:]), z8)

    gate_rows, down_rows = width // (ny * nz), ff // (ny * nz)
    lines = gate_rows * ff // 128
    columns = lambda v: v.reshape(-1, gate_rows, 128).transpose(1, 0, 2).reshape(gate_rows, -1)
    out_gate = columns(sum_a[:lines])
    out_up = jnp.concatenate([columns(sum_a[lines:]), columns(sum_b[lines:])], axis=1)
    out_down = sum_b[:lines].reshape(-1, down_rows, 128).transpose(1, 0, 2).reshape(down_rows, width)
    return grad_in, out_gate[None], out_up[None], out_down[None]


def solution(mesh):
    fine = Mesh(mesh.devices.reshape(4, 8, 4, 2), ("y", "z", "x", "core"))
    row = P(("y", "z", "x", "core"), None)
    weight = P(("x", "core"), None, None)
    summed = P(("x", "core"), ("y", "z"), None)
    return jax.shard_map(
        shards,
        mesh=fine,
        in_specs=(row, row, row, row, weight, weight, weight),
        out_specs=(row, summed, summed, summed),
        check_vma=False,
    )
```

```python
import functools

import jax
import jax.numpy as jnp
from jax import lax
from jax.experimental import pallas as pl
from jax.experimental.pallas import tpu as pltpu
from jax.sharding import Mesh
from jax.sharding import PartitionSpec as P

BF = jnp.bfloat16
F32 = jnp.float32
ROWS = (((0,), (0,)), ((), ()))
COLS = (((1,), (1,)), ((), ()))
VMEM_LIMIT = 36 * 1024 * 1024


def shift(value, axis, step):
    n = lax.axis_size(axis)
    return lax.ppermute(value, axis, [(i, (i + step) % n) for i in range(n)])


def add(*terms):
    total = terms[0].astype(F32)
    for term in terms[1:]:
        total = total + term.astype(F32)
    return total.astype(BF)


def params():
    return pltpu.CompilerParams(vmem_limit_bytes=VMEM_LIMIT)


def one_hots(experts_ref, metas):
    own, partner = experts_ref[0].astype(F32), experts_ref[1].astype(F32)
    tables = [m[...].astype(F32) for m in metas]
    hits, gates = [], []
    for table in tables:
        first, second = table[0:1], table[1:2]
        for expert in (own, partner):
            hits.append(jnp.where((first == expert) | (second == expert), 1.0, 0.0))
            gates.append(
                jnp.where(first == expert, table[2:3], 0.0)
                + jnp.where(second == expert, table[3:4], 0.0)
            )
    hit = jnp.concatenate(hits, axis=0)
    tokens = hit.shape[1]
    before = lax.broadcasted_iota(jnp.int32, (tokens, tokens), 0)
    after = lax.broadcasted_iota(jnp.int32, (tokens, tokens), 1)
    upper = jnp.where(before <= after, 1.0, 0.0).astype(BF)
    rank = jnp.dot(hit.astype(BF), upper, preferred_element_type=F32)
    place = jnp.where(hit > 0.0, rank - 1.0, -1.0)
    slots = lax.broadcasted_iota(jnp.int32, (tokens // 2, tokens), 0).astype(F32)
    result = []
    for chip in range(len(tables)):
        halves, scale = [], []
        for k in (2 * chip, 2 * chip + 1):
            half = jnp.where(place[k : k + 1] == slots, 1.0, 0.0)
            halves.append(half)
            scale.append(jnp.sum(half * gates[k], axis=1, keepdims=True))
        result.append((jnp.concatenate(halves, axis=0).astype(BF), jnp.concatenate(scale, axis=0)))
    return result


def fill_tables(experts_ref, metas, table_ref, scale_ref):
    @pl.when(pl.program_id(0) == 0)
    def _():
        for k, (table, scale) in enumerate(one_hots(experts_ref, metas)):
            table_ref[k] = table
            scale_ref[k] = jnp.broadcast_to(scale, scale_ref.shape[1:])


def table_scratch(tokens):
    return [pltpu.VMEM((4, tokens, tokens), BF), pltpu.VMEM((4, tokens, 128), F32)]


def gather_kernel(scaled, experts_ref, *refs):
    metas, (a, b, c, d0, d1), (own_ref, partner_ref) = refs[:4], refs[4:9], refs[9:11]
    table_ref, scale_ref = refs[11:]
    fill_tables(experts_ref, metas, table_ref, scale_ref)
    blocks = [a[...], b[...], c[...], jnp.concatenate([d0[...], d1[...]], axis=0)]
    for k in range(4):
        rows = jnp.dot(table_ref[k], blocks[k], preferred_element_type=F32)
        if scaled:
            rows = scale_ref[k][:, :1] * rows
        rows = rows.astype(BF)
        half = rows.shape[0] // 2
        own_ref[k * half : (k + 1) * half] = rows[:half]
        partner_ref[k * half : (k + 1) * half] = rows[half:]


def meta_specs(tokens):
    return [
        pl.BlockSpec((16, tokens), lambda i: (tokens // 16, 0)),
        pl.BlockSpec((16, tokens), lambda i: (tokens // 16, 0)),
        pl.BlockSpec((16, tokens), lambda i: (tokens // 16, 0)),
        pl.BlockSpec((16, tokens), lambda i: (tokens // 32, 0)),
    ]


def gather_rows(scaled, experts, metas, packets, tokens):
    width = packets[0].shape[1]
    tile = 512
    half = tokens // 2
    heights = (tokens, tokens, tokens, half, half)
    return pl.pallas_call(
        functools.partial(gather_kernel, scaled),
        grid=(width // tile,),
        in_specs=[pl.BlockSpec(memory_space=pltpu.SMEM)]
        + meta_specs(tokens)
        + [pl.BlockSpec((h, tile), lambda i: (0, i)) for h in heights],
        out_specs=[pl.BlockSpec((2 * tokens, tile), lambda i: (0, i))] * 2,
        out_shape=[jax.ShapeDtypeStruct((2 * tokens, width), BF)] * 2,
        scratch_shapes=table_scratch(tokens),
        compiler_params=params(),
        cost_estimate=pl.CostEstimate(
            flops=16 * tokens * tokens * width, bytes_accessed=16 * tokens * width, transcendentals=0
        ),
    )(experts, *metas, *packets)


def combine_kernel(experts_ref, *refs):
    metas, (own, partner), outs = refs[:4], refs[4:6], refs[6:10]
    table_ref, scale_ref = refs[10:]
    fill_tables(experts_ref, metas, table_ref, scale_ref)
    for k in range(4):
        table = table_ref[k]
        half = table.shape[0] // 2
        part = slice(k * half, (k + 1) * half)
        terms = jnp.concatenate([own[part], partner[part]], axis=0)
        outs[k][...] = lax.dot_general(table, terms, ROWS, preferred_element_type=F32).astype(BF)


def combine(experts, metas, own, partner, tokens):
    width = own.shape[1]
    tile = 512
    return pl.pallas_call(
        combine_kernel,
        grid=(width // tile,),
        in_specs=[pl.BlockSpec(memory_space=pltpu.SMEM)]
        + meta_specs(tokens)
        + [pl.BlockSpec((2 * tokens, tile), lambda i: (0, i))] * 2,
        out_specs=[pl.BlockSpec((tokens, tile), lambda i: (0, i))] * 4,
        out_shape=[jax.ShapeDtypeStruct((tokens, width), BF)] * 4,
        scratch_shapes=table_scratch(tokens),
        compiler_params=params(),
        cost_estimate=pl.CostEstimate(
            flops=tokens * width, bytes_accessed=tokens * width, transcendentals=0
        ),
    )(experts, *metas, own, partner)


def forward_kernel(xa, xb, gate_w, up_w, hidden, to_gate, to_up):
    half = xa.shape[0]
    for k, x in enumerate((xa, xb)):
        rows = slice(k * half, (k + 1) * half)
        pre_gate = jnp.dot(x[...], gate_w[0], preferred_element_type=F32)
        pre_up = jnp.dot(x[...], up_w[0], preferred_element_type=F32)
        sigmoid = jax.nn.sigmoid(pre_gate)
        silu = pre_gate * sigmoid
        hidden[rows] = (silu * pre_up).astype(BF)
        to_gate[rows] = pre_up * sigmoid * (1.0 + pre_gate * (1.0 - sigmoid))
        to_up[rows] = silu


def forward(xa, xb, gate_w, up_w):
    half, width = xa.shape
    ff = gate_w.shape[2]
    tile = 256
    whole = pl.BlockSpec((half, width), lambda i: (0, 0))
    weight = pl.BlockSpec((1, width, tile), lambda i: (0, 0, i))
    out = pl.BlockSpec((2 * half, tile), lambda i: (0, i))
    return pl.pallas_call(
        forward_kernel,
        grid=(ff // tile,),
        in_specs=[whole, whole, weight, weight],
        out_specs=[out] * 3,
        out_shape=[
            jax.ShapeDtypeStruct((2 * half, ff), BF),
            jax.ShapeDtypeStruct((2 * half, ff), F32),
            jax.ShapeDtypeStruct((2 * half, ff), F32),
        ],
        compiler_params=params(),
        cost_estimate=pl.CostEstimate(
            flops=8 * half * width * ff, bytes_accessed=4 * width * ff + 24 * half * ff, transcendentals=2 * half * ff
        ),
    )(xa, xb, gate_w, up_w)


def down_kernel(ny, nz, down_rows, gate_rows, me_ref, *refs):
    xa, xb, ga, gb, hidden, to_gate, to_up, down_w, grad_gate, grad_up, part, right, left = refs
    step = pl.program_id(0)
    steps_down = ny // 2
    tile = down_w.shape[1]
    width = xa.shape[1]
    rel = lambda z: lax.rem(z - me_ref[1] + nz, nz)

    @pl.when(step < steps_down)
    def _():
        columns = pl.ds(pl.multiple_of(step * tile, 128), tile)
        grad = jnp.concatenate([ga[...], gb[...]], axis=0)
        grad_hidden = lax.dot_general(grad, down_w[0], COLS, preferred_element_type=F32)
        grad_gate[:, columns] = (grad_hidden * to_gate[...]).astype(BF)
        grad_up[:, columns] = (grad_hidden * to_up[...]).astype(BF)
        block = lax.dot_general(hidden[...], grad, ROWS, preferred_element_type=F32)
        for y in range(2):
            for z in range(nz):
                rows = block[(y * nz + z) * down_rows : (y * nz + z + 1) * down_rows]
                for c in range(width // 256):
                    pair = [rows[:, c * 256 : c * 256 + 128], rows[:, c * 256 + 128 : c * 256 + 256]]
                    pair = jnp.concatenate(pair, axis=0).astype(BF)
                    part[rel(z), 2 * step + y, c * 2 * down_rows : (c + 1) * 2 * down_rows] = pair

    @pl.when(step == steps_down)
    def _():
        half = grad_up.shape[1] // 2
        lines = down_rows * width // 128
        deep = width // ny
        for y in range(ny):
            x = jnp.concatenate(
                [xa[:, y * deep : (y + 1) * deep], xb[:, y * deep : (y + 1) * deep]], axis=0
            )
            block = lax.dot_general(x, grad_up[:, half:], ROWS, preferred_element_type=F32)
            for z in range(nz):
                for c in range(half // 128):
                    rows = block[z * gate_rows : (z + 1) * gate_rows, c * 128 : (c + 1) * 128]
                    at = lines + c * gate_rows
                    part[rel(z), y, at : at + gate_rows] = rows.astype(BF)
        near, far, h = nz // 2 - 1, nz // 2, ny // 2
        right[:h], right[h:] = part[far, :h], part[near, h:]
        left[:h], left[h:] = part[nz - near, :h], part[far, h:]


def down_grads(me, xa, xb, ga, gb, hidden, to_gate, to_up, down_w, ny, nz):
    half, width = xa.shape
    ff = hidden.shape[1]
    down_rows, gate_rows = ff // (ny * nz), width // (ny * nz)
    lines = 3 * gate_rows * ff // 256
    down = ny // 2
    tile = ff // down
    first = lambda i: jnp.minimum(i, down - 1)
    g_spec = pl.BlockSpec((half, width), lambda i, m: (0, 0))
    f_spec = pl.BlockSpec((2 * half, tile), lambda i, m: (0, first(i)))
    grad_spec = pl.BlockSpec((2 * half, ff), lambda i, m: (0, 0))
    sent = pl.BlockSpec((ny, lines, 128), lambda i, m: (0, 0, 0))
    return pl.pallas_call(
        functools.partial(down_kernel, ny, nz, down_rows, gate_rows),
        grid_spec=pltpu.PrefetchScalarGridSpec(
            num_scalar_prefetch=1,
            grid=(down + 1,),
            in_specs=[g_spec] * 4
            + [f_spec] * 3
            + [pl.BlockSpec((1, tile, width), lambda i, m: (0, first(i), 0))],
            out_specs=[
                grad_spec,
                grad_spec,
                pl.BlockSpec((nz, ny, lines, 128), lambda i, m: (0, 0, 0, 0)),
                sent,
                sent,
            ],
        ),
        out_shape=[
            jax.ShapeDtypeStruct((2 * half, ff), BF),
            jax.ShapeDtypeStruct((2 * half, ff), BF),
            jax.ShapeDtypeStruct((nz, ny, lines, 128), BF),
            jax.ShapeDtypeStruct((ny, lines, 128), BF),
            jax.ShapeDtypeStruct((ny, lines, 128), BF),
        ],
        compiler_params=params(),
        cost_estimate=pl.CostEstimate(
            flops=10 * half * width * ff, bytes_accessed=4 * width * ff + 8 * half * width, transcendentals=0
        ),
    )(me, xa, xb, ga, gb, hidden, to_gate, to_up, down_w)


def gate_kernel(nz, gate_rows, me_ref, xa, xb, grad_gate, grad_up, *refs):
    outs, grads = refs[:-1], refs[-1]
    ff = grad_gate.shape[1]

    @pl.when(pl.program_id(0) == 0)
    def _():
        grads[:, :ff] = grad_gate[...]
        grads[:, ff:] = grad_up[:, : ff // 2]

    x = jnp.concatenate([xa[...], xb[...]], axis=0)
    block = lax.dot_general(x, grads[...], ROWS, preferred_element_type=F32)
    each = nz // len(outs)
    for z in range(nz):
        for c in range(grads.shape[1] // 128):
            rows = block[z * gate_rows : (z + 1) * gate_rows, c * 128 : (c + 1) * 128]
            outs[z // each][0, z % each, c * gate_rows : (c + 1) * gate_rows] = rows.astype(BF)


def gate_grads(me, xa, xb, grad_gate, grad_up, ny, nz, far):
    half, width = xa.shape
    ff = grad_gate.shape[1]
    gate_rows = width // (ny * nz)
    lines = 3 * gate_rows * ff // 256
    steps = 1 if far else 3
    turn = lambda i: 2 if far else jnp.where(i == 0, 1, jnp.where(i == 1, 3, 0))
    place = lambda i: 0 if far else jnp.minimum(turn(i), 2)
    x_spec = pl.BlockSpec((half, width // ny), lambda i, m: (0, lax.rem(m[0] + turn(i), ny)))
    grad_spec = pl.BlockSpec((2 * half, ff), lambda i, m: (0, 0))
    outs = 2 if far else 1
    return pl.pallas_call(
        functools.partial(gate_kernel, nz, gate_rows),
        grid_spec=pltpu.PrefetchScalarGridSpec(
            num_scalar_prefetch=1,
            grid=(steps,),
            in_specs=[x_spec, x_spec, grad_spec, grad_spec],
            out_specs=[pl.BlockSpec((1, nz // outs, lines, 128), lambda i, m: (place(i), 0, 0, 0))] * outs,
            scratch_shapes=[pltpu.VMEM((2 * half, ff + ff // 2), BF)],
        ),
        out_shape=[jax.ShapeDtypeStruct((steps, nz // outs, lines, 128), BF)] * outs,
        compiler_params=params(),
        cost_estimate=pl.CostEstimate(
            flops=2 * steps * half * width * ff, bytes_accessed=steps * (half * width + width * ff), transcendentals=0
        ),
    )(me, xa, xb, grad_gate, grad_up)


def terms_kernel(grad_gate, grad_up, gate_w, up_w, first, second):
    half = first.shape[0]
    total = lax.dot_general(grad_gate[...], gate_w[0], COLS, preferred_element_type=F32)
    total = total + lax.dot_general(grad_up[...], up_w[0], COLS, preferred_element_type=F32)
    total = total.astype(BF)
    first[...] = total[:half]
    second[...] = total[half:]


def input_terms(grad_gate, grad_up, gate_w, up_w):
    slots, ff = grad_gate.shape
    width = gate_w.shape[1]
    tile = 512
    grad = pl.BlockSpec((slots, ff), lambda i: (0, 0))
    weight = pl.BlockSpec((1, tile, ff), lambda i: (0, i, 0))
    out = pl.BlockSpec((slots // 2, tile), lambda i: (0, i))
    return pl.pallas_call(
        terms_kernel,
        grid=(width // tile,),
        in_specs=[grad, grad, weight, weight],
        out_specs=[out, out],
        out_shape=[jax.ShapeDtypeStruct((slots // 2, width), BF)] * 2,
        compiler_params=params(),
        cost_estimate=pl.CostEstimate(
            flops=slots * ff, bytes_accessed=slots * ff, transcendentals=0
        ),
    )(grad_gate, grad_up, gate_w, up_w)


def cat(first, second):
    return jnp.concatenate([first, second], axis=0)


class Blocks:
    def __init__(self, value, axis, counted_from_here):
        self.value, self.axis, self.n = value, axis, lax.axis_size(axis)
        self.half = value.shape[1] // 2
        self.start = 0 if counted_from_here else lax.axis_index(axis)

    def block(self, k):
        if self.value.shape[0] == self.n - 1:
            return self.value[min(k % self.n, self.n - 2)]
        return lax.dynamic_index_in_dim(self.value, (self.start + k + self.n) % self.n, 0, keepdims=False)

    def low(self, k):
        return self.block(k)[: self.half]

    def high(self, k):
        return self.block(k)[self.half :]

    def send(self, right, left):
        return shift(right, self.axis, 1), shift(left, self.axis, -1)

    def total(self, *pairs):
        result = self.block(0).astype(F32)
        for low, high in pairs:
            result = result + cat(low, high).astype(F32)
        return result


def shards(inputs, grad_out, expert_ids, gate_probs, w_gate, w_up, w_down):
    tokens, width = inputs.shape
    ff = w_gate.shape[2]
    ny, nz = lax.axis_size("y"), lax.axis_size("z")
    half = tokens // 2
    chip, core = lax.axis_index("x"), lax.axis_index("core")
    experts = jnp.stack([2 * chip + core, 2 * chip + 1 - core]).astype(jnp.int32)
    me = jnp.stack([lax.axis_index("y"), lax.axis_index("z")]).astype(jnp.int32)
    fence = lax.optimization_barrier

    table = jnp.concatenate([expert_ids.T.astype(BF), gate_probs.T], axis=0)
    table = jnp.pad(table, ((0, 12), (0, width - tokens)))
    packet = jnp.concatenate([inputs, table], axis=0)

    x_left, x_right = shift(packet, "x", 1), shift(packet, "x", -1)
    x_left, x_right, later = fence((x_left, x_right, grad_out))
    g_left, g_right = shift(later, "x", 1), shift(later, "x", -1)
    x_low, x_high = shift(x_left[:half], "x", 1), shift(x_right[half:], "x", -1)
    g_low, g_high = shift(g_left[:half], "x", 1), shift(g_right[half:], "x", -1)
    metas = (packet, x_left, x_right, x_high)

    xa, x_partner = gather_rows(False, experts, metas, (packet, x_left, x_right, x_low, x_high), tokens)
    xb = shift(x_partner, "core", 1)
    hidden, to_gate, to_up = forward(xa, xb, w_gate, w_up)
    ga, g_partner = gather_rows(True, experts, metas, (grad_out, g_left, g_right, g_low, g_high), tokens)
    gb = shift(g_partner, "core", 1)
    grad_gate, grad_up, part_b, b_right, b_left = down_grads(
        me, xa, xb, ga, gb, hidden, to_gate, to_up, w_down, ny, nz
    )

    b = Blocks(part_b, "z", True)
    h = b.half
    a_low, a_high = gate_grads(me, xa, xb, grad_gate, grad_up, ny, nz, True)
    b_right, b_left, a_low, a_high, grads = fence((b_right, b_left, a_low[0], a_high[0], (grad_gate, grad_up)))
    z1 = b.send(b_right, b_left)
    y1 = shift(a_low, "y", 1), shift(a_high, "y", -1)
    (part_a,) = gate_grads(me, xa, xb, *grads, ny, nz, False)
    terms = input_terms(*grads, w_gate, w_up)

    ops = (add(cat(b.low(3), b.high(2)), z1[0]), add(cat(b.low(-2), b.high(-3)), z1[1]))
    ops, (term_own, term_other), part_a = fence((ops, terms, part_a))
    a = Blocks(part_a, "y", True)
    z2 = b.send(*ops)
    term_partner = shift(term_other, "core", 1)

    ops, y1, _ = fence(((a.high(1), a.low(-1)), y1, z1))
    y2 = a.send(*ops)

    ops = (add(cat(b.low(2), b.high(1)), z2[0]), add(cat(b.low(-1), b.high(-2)), z2[1]))
    ops, (term_own, term_partner) = fence((ops, (term_own, term_partner)))
    z3 = b.send(*ops)
    blocks = combine(experts, metas, term_own, term_partner, tokens)

    ops, y2, _ = fence(((add(a.low(1), y1[0]), add(a.high(-1), y1[1])), y2, z2))
    y3 = a.send(*ops)

    ops = (add(b.low(1), z3[0][:h]), add(b.high(-1), z3[1][h:]))
    z4 = b.send(*fence(ops))

    a = Blocks(a.total((y2[1], y2[0]), y3).astype(BF), "z", False)
    u = a.half
    ops = (cat(a.low(4), a.high(3)), cat(a.low(-3), a.high(4)))
    ops, _ = fence((ops, z3))
    z5 = a.send(*ops)

    b = Blocks(b.total((z3[1][:h], z3[0][h:]), z4).astype(BF), "y", False)
    ops = (cat(b.low(2), b.high(1)), cat(b.low(-1), b.high(2)))
    ops, (mine, for_left, for_right, for_far) = fence((ops, blocks))
    y4 = b.send(*ops)
    from_far = shift(for_far, "x", 2)

    ops = (add(cat(a.low(3), a.high(2)), z5[0]), add(cat(a.low(-2), a.high(-3)), z5[1]))
    ops, _ = fence((ops, z4))
    z6 = a.send(*ops)

    y5 = b.send(*fence((add(b.low(1), y4[0][:u]), add(b.high(-1), y4[1][u:]))))
    ops = (add(cat(a.low(2), a.high(1)), z6[0]), add(cat(a.low(-1), a.high(-2)), z6[1]))
    ops, for_left, for_right = fence((ops, for_left, for_right))
    z7 = a.send(*ops)
    from_right, from_left = shift(for_left, "x", -1), shift(for_right, "x", 1)
    z8 = a.send(*fence((add(a.low(1), z7[0][:u]), add(a.high(-1), z7[1][u:]))))
    grad_in = add(mine, from_far, from_right, from_left)
    sum_b = b.total((y4[1][:u], y4[0][u:]), y5)
    sum_a = a.total((z7[1][:u], z7[0][u:]), z8)

    gate_rows, down_rows = width // (ny * nz), ff // (ny * nz)
    lines = gate_rows * ff // 128
    columns = lambda v: v.reshape(-1, gate_rows, 128).transpose(1, 0, 2).reshape(gate_rows, -1)
    out_gate = columns(sum_a[:lines])
    out_up = jnp.concatenate([columns(sum_a[lines:]), columns(sum_b[lines:])], axis=1)
    out_down = sum_b[:lines].reshape(-1, down_rows, 128).transpose(1, 0, 2).reshape(down_rows, width)
    return grad_in, out_gate[None], out_up[None], out_down[None]


def solution(mesh):
    fine = Mesh(mesh.devices.reshape(4, 8, 4, 2), ("y", "z", "x", "core"))
    row = P(("y", "z", "x", "core"), None)
    weight = P(("x", "core"), None, None)
    summed = P(("x", "core"), ("y", "z"), None)
    return jax.shard_map(
        shards,
        mesh=fine,
        in_specs=(row, row, row, row, weight, weight, weight),
        out_specs=(row, summed, summed, summed),
        check_vma=False,
    )
```

```python
import functools

import jax
import jax.numpy as jnp
from jax import lax
from jax.experimental import pallas as pl
from jax.experimental.pallas import tpu as pltpu
from jax.sharding import Mesh
from jax.sharding import PartitionSpec as P

BF = jnp.bfloat16
F32 = jnp.float32
ROWS = (((0,), (0,)), ((), ()))
COLS = (((1,), (1,)), ((), ()))
VMEM_LIMIT = 36 * 1024 * 1024


def shift(value, axis, step):
    n = lax.axis_size(axis)
    return lax.ppermute(value, axis, [(i, (i + step) % n) for i in range(n)])


def add(*terms):
    total = terms[0].astype(F32)
    for term in terms[1:]:
        total = total + term.astype(F32)
    return total.astype(BF)


def params():
    return pltpu.CompilerParams(vmem_limit_bytes=VMEM_LIMIT)


def one_hots(experts_ref, metas):
    own, partner = experts_ref[0].astype(F32), experts_ref[1].astype(F32)
    tables = [m[...].astype(F32) for m in metas]
    hits, gates = [], []
    for table in tables:
        first, second = table[0:1], table[1:2]
        for expert in (own, partner):
            hits.append(jnp.where((first == expert) | (second == expert), 1.0, 0.0))
            gates.append(
                jnp.where(first == expert, table[2:3], 0.0)
                + jnp.where(second == expert, table[3:4], 0.0)
            )
    hit = jnp.concatenate(hits, axis=0)
    tokens = hit.shape[1]
    before = lax.broadcasted_iota(jnp.int32, (tokens, tokens), 0)
    after = lax.broadcasted_iota(jnp.int32, (tokens, tokens), 1)
    upper = jnp.where(before <= after, 1.0, 0.0).astype(BF)
    rank = jnp.dot(hit.astype(BF), upper, preferred_element_type=F32)
    place = jnp.where(hit > 0.0, rank - 1.0, -1.0)
    slots = lax.broadcasted_iota(jnp.int32, (tokens // 2, tokens), 0).astype(F32)
    result = []
    for chip in range(len(tables)):
        halves, scale = [], []
        for k in (2 * chip, 2 * chip + 1):
            half = jnp.where(place[k : k + 1] == slots, 1.0, 0.0)
            halves.append(half)
            scale.append(jnp.sum(half * gates[k], axis=1, keepdims=True))
        result.append((jnp.concatenate(halves, axis=0).astype(BF), jnp.concatenate(scale, axis=0)))
    return result


def fill_tables(experts_ref, metas, table_ref, scale_ref):
    @pl.when(pl.program_id(0) == 0)
    def _():
        for k, (table, scale) in enumerate(one_hots(experts_ref, metas)):
            table_ref[k] = table
            scale_ref[k] = jnp.broadcast_to(scale, scale_ref.shape[1:])


def table_scratch(tokens):
    return [pltpu.VMEM((4, tokens, tokens), BF), pltpu.VMEM((4, tokens, 128), F32)]


def gather_kernel(scaled, experts_ref, *refs):
    metas, (a, b, c, d0, d1), (own_ref, partner_ref) = refs[:4], refs[4:9], refs[9:11]
    table_ref, scale_ref = refs[11:]
    fill_tables(experts_ref, metas, table_ref, scale_ref)
    blocks = [a[...], b[...], c[...], jnp.concatenate([d0[...], d1[...]], axis=0)]
    for k in range(4):
        rows = jnp.dot(table_ref[k], blocks[k], preferred_element_type=F32)
        if scaled:
            rows = scale_ref[k][:, :1] * rows
        rows = rows.astype(BF)
        half = rows.shape[0] // 2
        own_ref[k * half : (k + 1) * half] = rows[:half]
        partner_ref[k * half : (k + 1) * half] = rows[half:]


def meta_specs(tokens):
    return [
        pl.BlockSpec((16, tokens), lambda i: (tokens // 16, 0)),
        pl.BlockSpec((16, tokens), lambda i: (tokens // 16, 0)),
        pl.BlockSpec((16, tokens), lambda i: (tokens // 16, 0)),
        pl.BlockSpec((16, tokens), lambda i: (tokens // 32, 0)),
    ]


def gather_rows(scaled, experts, metas, packets, tokens):
    width = packets[0].shape[1]
    tile = 512
    half = tokens // 2
    heights = (tokens, tokens, tokens, half, half)
    return pl.pallas_call(
        functools.partial(gather_kernel, scaled),
        grid=(width // tile,),
        in_specs=[pl.BlockSpec(memory_space=pltpu.SMEM)]
        + meta_specs(tokens)
        + [pl.BlockSpec((h, tile), lambda i: (0, i)) for h in heights],
        out_specs=[pl.BlockSpec((2 * tokens, tile), lambda i: (0, i))] * 2,
        out_shape=[jax.ShapeDtypeStruct((2 * tokens, width), BF)] * 2,
        scratch_shapes=table_scratch(tokens),
        compiler_params=params(),
        cost_estimate=pl.CostEstimate(
            flops=16 * tokens * tokens * width, bytes_accessed=16 * tokens * width, transcendentals=0
        ),
    )(experts, *metas, *packets)


def combine_kernel(experts_ref, *refs):
    metas, (own, partner), outs = refs[:4], refs[4:6], refs[6:10]
    table_ref, scale_ref = refs[10:]
    fill_tables(experts_ref, metas, table_ref, scale_ref)
    for k in range(4):
        table = table_ref[k]
        half = table.shape[0] // 2
        part = slice(k * half, (k + 1) * half)
        terms = jnp.concatenate([own[part], partner[part]], axis=0)
        outs[k][...] = lax.dot_general(table, terms, ROWS, preferred_element_type=F32).astype(BF)


def combine(experts, metas, own, partner, tokens):
    width = own.shape[1]
    tile = 512
    return pl.pallas_call(
        combine_kernel,
        grid=(width // tile,),
        in_specs=[pl.BlockSpec(memory_space=pltpu.SMEM)]
        + meta_specs(tokens)
        + [pl.BlockSpec((2 * tokens, tile), lambda i: (0, i))] * 2,
        out_specs=[pl.BlockSpec((tokens, tile), lambda i: (0, i))] * 4,
        out_shape=[jax.ShapeDtypeStruct((tokens, width), BF)] * 4,
        scratch_shapes=table_scratch(tokens),
        compiler_params=params(),
        cost_estimate=pl.CostEstimate(
            flops=tokens * width, bytes_accessed=tokens * width, transcendentals=0
        ),
    )(experts, *metas, own, partner)


def forward_kernel(xa, xb, gate_w, up_w, hidden, to_gate, to_up):
    half = xa.shape[0]
    for k, x in enumerate((xa, xb)):
        rows = slice(k * half, (k + 1) * half)
        pre_gate = jnp.dot(x[...], gate_w[0], preferred_element_type=F32)
        pre_up = jnp.dot(x[...], up_w[0], preferred_element_type=F32)
        sigmoid = jax.nn.sigmoid(pre_gate)
        silu = pre_gate * sigmoid
        hidden[rows] = (silu * pre_up).astype(BF)
        to_gate[rows] = pre_up * sigmoid * (1.0 + pre_gate * (1.0 - sigmoid))
        to_up[rows] = silu


def forward(xa, xb, gate_w, up_w):
    half, width = xa.shape
    ff = gate_w.shape[2]
    tile = 256
    whole = pl.BlockSpec((half, width), lambda i: (0, 0))
    weight = pl.BlockSpec((1, width, tile), lambda i: (0, 0, i))
    out = pl.BlockSpec((2 * half, tile), lambda i: (0, i))
    return pl.pallas_call(
        forward_kernel,
        grid=(ff // tile,),
        in_specs=[whole, whole, weight, weight],
        out_specs=[out] * 3,
        out_shape=[
            jax.ShapeDtypeStruct((2 * half, ff), BF),
            jax.ShapeDtypeStruct((2 * half, ff), F32),
            jax.ShapeDtypeStruct((2 * half, ff), F32),
        ],
        compiler_params=params(),
        cost_estimate=pl.CostEstimate(
            flops=8 * half * width * ff, bytes_accessed=4 * width * ff + 24 * half * ff, transcendentals=2 * half * ff
        ),
    )(xa, xb, gate_w, up_w)


def down_kernel(ny, nz, down_rows, gate_rows, me_ref, *refs):
    xa, xb, ga, gb, hidden, to_gate, to_up, down_w, grad_gate, grad_up, part, right, left = refs
    step = pl.program_id(0)
    steps_down = ny // 2
    tile = down_w.shape[1]
    width = xa.shape[1]
    rel = lambda z: lax.rem(z - me_ref[1] + nz, nz)

    @pl.when(step < steps_down)
    def _():
        columns = pl.ds(pl.multiple_of(step * tile, 128), tile)
        grad = jnp.concatenate([ga[...], gb[...]], axis=0)
        grad_hidden = lax.dot_general(grad, down_w[0], COLS, preferred_element_type=F32)
        grad_gate[:, columns] = (grad_hidden * to_gate[...]).astype(BF)
        grad_up[:, columns] = (grad_hidden * to_up[...]).astype(BF)
        block = lax.dot_general(hidden[...], grad, ROWS, preferred_element_type=F32)
        for y in range(2):
            for z in range(nz):
                rows = block[(y * nz + z) * down_rows : (y * nz + z + 1) * down_rows]
                for c in range(width // 256):
                    pair = [rows[:, c * 256 : c * 256 + 128], rows[:, c * 256 + 128 : c * 256 + 256]]
                    pair = jnp.concatenate(pair, axis=0).astype(BF)
                    part[rel(z), 2 * step + y, c * 2 * down_rows : (c + 1) * 2 * down_rows] = pair

    @pl.when(step == steps_down)
    def _():
        half = grad_up.shape[1] // 2
        lines = down_rows * width // 128
        deep = width // ny
        for y in range(ny):
            x = jnp.concatenate(
                [xa[:, y * deep : (y + 1) * deep], xb[:, y * deep : (y + 1) * deep]], axis=0
            )
            block = lax.dot_general(x, grad_up[:, half:], ROWS, preferred_element_type=F32)
            for z in range(nz):
                for c in range(half // 128):
                    rows = block[z * gate_rows : (z + 1) * gate_rows, c * 128 : (c + 1) * 128]
                    at = lines + c * gate_rows
                    part[rel(z), y, at : at + gate_rows] = rows.astype(BF)
        near, far, h = nz // 2 - 1, nz // 2, ny // 2
        right[:h], right[h:] = part[far, :h], part[near, h:]
        left[:h], left[h:] = part[nz - near, :h], part[far, h:]


def down_grads(me, xa, xb, ga, gb, hidden, to_gate, to_up, down_w, ny, nz):
    half, width = xa.shape
    ff = hidden.shape[1]
    down_rows, gate_rows = ff // (ny * nz), width // (ny * nz)
    lines = 3 * gate_rows * ff // 256
    down = ny // 2
    tile = ff // down
    first = lambda i: jnp.minimum(i, down - 1)
    g_spec = pl.BlockSpec((half, width), lambda i, m: (0, 0))
    f_spec = pl.BlockSpec((2 * half, tile), lambda i, m: (0, first(i)))
    grad_spec = pl.BlockSpec((2 * half, ff), lambda i, m: (0, 0))
    sent = pl.BlockSpec((ny, lines, 128), lambda i, m: (0, 0, 0))
    return pl.pallas_call(
        functools.partial(down_kernel, ny, nz, down_rows, gate_rows),
        grid_spec=pltpu.PrefetchScalarGridSpec(
            num_scalar_prefetch=1,
            grid=(down + 1,),
            in_specs=[g_spec] * 4
            + [f_spec] * 3
            + [pl.BlockSpec((1, tile, width), lambda i, m: (0, first(i), 0))],
            out_specs=[
                grad_spec,
                grad_spec,
                pl.BlockSpec((nz, ny, lines, 128), lambda i, m: (0, 0, 0, 0)),
                sent,
                sent,
            ],
        ),
        out_shape=[
            jax.ShapeDtypeStruct((2 * half, ff), BF),
            jax.ShapeDtypeStruct((2 * half, ff), BF),
            jax.ShapeDtypeStruct((nz, ny, lines, 128), BF),
            jax.ShapeDtypeStruct((ny, lines, 128), BF),
            jax.ShapeDtypeStruct((ny, lines, 128), BF),
        ],
        compiler_params=params(),
        cost_estimate=pl.CostEstimate(
            flops=10 * half * width * ff, bytes_accessed=4 * width * ff + 8 * half * width, transcendentals=0
        ),
    )(me, xa, xb, ga, gb, hidden, to_gate, to_up, down_w)


def gate_kernel(nz, gate_rows, me_ref, xa, xb, grad_gate, grad_up, *refs):
    outs, grads = refs[:-1], refs[-1]
    ff = grad_gate.shape[1]

    @pl.when(pl.program_id(0) == 0)
    def _():
        grads[:, :ff] = grad_gate[...]
        grads[:, ff:] = grad_up[:, : ff // 2]

    x = jnp.concatenate([xa[...], xb[...]], axis=0)
    block = lax.dot_general(x, grads[...], ROWS, preferred_element_type=F32)
    each = nz // len(outs)
    for z in range(nz):
        for c in range(grads.shape[1] // 128):
            rows = block[z * gate_rows : (z + 1) * gate_rows, c * 128 : (c + 1) * 128]
            outs[z // each][0, z % each, c * gate_rows : (c + 1) * gate_rows] = rows.astype(BF)


def gate_grads(me, xa, xb, grad_gate, grad_up, ny, nz, far):
    half, width = xa.shape
    ff = grad_gate.shape[1]
    gate_rows = width // (ny * nz)
    lines = 3 * gate_rows * ff // 256
    steps = 1 if far else 3
    turn = lambda i: 2 if far else jnp.where(i == 0, 1, jnp.where(i == 1, 3, 0))
    place = lambda i: 0 if far else jnp.minimum(turn(i), 2)
    x_spec = pl.BlockSpec((half, width // ny), lambda i, m: (0, lax.rem(m[0] + turn(i), ny)))
    grad_spec = pl.BlockSpec((2 * half, ff), lambda i, m: (0, 0))
    outs = 2 if far else 1
    return pl.pallas_call(
        functools.partial(gate_kernel, nz, gate_rows),
        grid_spec=pltpu.PrefetchScalarGridSpec(
            num_scalar_prefetch=1,
            grid=(steps,),
            in_specs=[x_spec, x_spec, grad_spec, grad_spec],
            out_specs=[pl.BlockSpec((1, nz // outs, lines, 128), lambda i, m: (place(i), 0, 0, 0))] * outs,
            scratch_shapes=[pltpu.VMEM((2 * half, ff + ff // 2), BF)],
        ),
        out_shape=[jax.ShapeDtypeStruct((steps, nz // outs, lines, 128), BF)] * outs,
        compiler_params=params(),
        cost_estimate=pl.CostEstimate(
            flops=2 * steps * half * width * ff, bytes_accessed=steps * (half * width + width * ff), transcendentals=0
        ),
    )(me, xa, xb, grad_gate, grad_up)


def terms_kernel(grad_gate, grad_up, gate_w, up_w, first, second):
    half = first.shape[0]
    total = lax.dot_general(grad_gate[...], gate_w[0], COLS, preferred_element_type=F32)
    total = total + lax.dot_general(grad_up[...], up_w[0], COLS, preferred_element_type=F32)
    total = total.astype(BF)
    first[...] = total[:half]
    second[...] = total[half:]


def input_terms(grad_gate, grad_up, gate_w, up_w):
    slots, ff = grad_gate.shape
    width = gate_w.shape[1]
    tile = 512
    grad = pl.BlockSpec((slots, ff), lambda i: (0, 0))
    weight = pl.BlockSpec((1, tile, ff), lambda i: (0, i, 0))
    out = pl.BlockSpec((slots // 2, tile), lambda i: (0, i))
    return pl.pallas_call(
        terms_kernel,
        grid=(width // tile,),
        in_specs=[grad, grad, weight, weight],
        out_specs=[out, out],
        out_shape=[jax.ShapeDtypeStruct((slots // 2, width), BF)] * 2,
        compiler_params=params(),
        cost_estimate=pl.CostEstimate(
            flops=slots * ff, bytes_accessed=slots * ff, transcendentals=0
        ),
    )(grad_gate, grad_up, gate_w, up_w)


def cat(first, second):
    return jnp.concatenate([first, second], axis=0)


class Blocks:
    def __init__(self, value, axis, counted_from_here):
        self.value, self.axis, self.n = value, axis, lax.axis_size(axis)
        self.half = value.shape[1] // 2
        self.start = 0 if counted_from_here else lax.axis_index(axis)

    def block(self, k):
        if self.value.shape[0] == self.n - 1:
            return self.value[min(k % self.n, self.n - 2)]
        return lax.dynamic_index_in_dim(self.value, (self.start + k + self.n) % self.n, 0, keepdims=False)

    def low(self, k):
        return self.block(k)[: self.half]

    def high(self, k):
        return self.block(k)[self.half :]

    def send(self, right, left):
        return shift(right, self.axis, 1), shift(left, self.axis, -1)

    def total(self, *pairs):
        result = self.block(0).astype(F32)
        for low, high in pairs:
            result = result + cat(low, high).astype(F32)
        return result


def shards(inputs, grad_out, expert_ids, gate_probs, w_gate, w_up, w_down):
    tokens, width = inputs.shape
    ff = w_gate.shape[2]
    ny, nz = lax.axis_size("y"), lax.axis_size("z")
    half = tokens // 2
    chip, core = lax.axis_index("x"), lax.axis_index("core")
    experts = jnp.stack([2 * chip + core, 2 * chip + 1 - core]).astype(jnp.int32)
    me = jnp.stack([lax.axis_index("y"), lax.axis_index("z")]).astype(jnp.int32)
    fence = lax.optimization_barrier

    table = jnp.concatenate([expert_ids.T.astype(BF), gate_probs.T], axis=0)
    table = jnp.pad(table, ((0, 12), (0, width - tokens)))
    packet = jnp.concatenate([inputs, table], axis=0)

    x_left, x_right = shift(packet, "x", 1), shift(packet, "x", -1)
    g_left, g_right = shift(grad_out, "x", 1), shift(grad_out, "x", -1)
    x_low, x_high = shift(x_left[:half], "x", 1), shift(x_right[half:], "x", -1)
    g_low, g_high = shift(g_left[:half], "x", 1), shift(g_right[half:], "x", -1)
    metas = (packet, x_left, x_right, x_high)

    xa, x_partner = gather_rows(False, experts, metas, (packet, x_left, x_right, x_low, x_high), tokens)
    xb = shift(x_partner, "core", 1)
    hidden, to_gate, to_up = forward(xa, xb, w_gate, w_up)
    ga, g_partner = gather_rows(True, experts, metas, (grad_out, g_left, g_right, g_low, g_high), tokens)
    gb = shift(g_partner, "core", 1)
    grad_gate, grad_up, part_b, b_right, b_left = down_grads(
        me, xa, xb, ga, gb, hidden, to_gate, to_up, w_down, ny, nz
    )

    b = Blocks(part_b, "z", True)
    h = b.half
    a_low, a_high = gate_grads(me, xa, xb, grad_gate, grad_up, ny, nz, True)
    b_right, b_left, a_low, a_high, grads = fence((b_right, b_left, a_low[0], a_high[0], (grad_gate, grad_up)))
    z1 = b.send(b_right, b_left)
    y1 = shift(a_low, "y", 1), shift(a_high, "y", -1)
    (part_a,) = gate_grads(me, xa, xb, *grads, ny, nz, False)
    terms = input_terms(*grads, w_gate, w_up)

    ops = (add(cat(b.low(3), b.high(2)), z1[0]), add(cat(b.low(-2), b.high(-3)), z1[1]))
    ops, (term_own, term_other), part_a = fence((ops, terms, part_a))
    a = Blocks(part_a, "y", True)
    z2 = b.send(*ops)
    term_partner = shift(term_other, "core", 1)

    ops, y1, _ = fence(((a.high(1), a.low(-1)), y1, z1))
    y2 = a.send(*ops)

    ops = (add(cat(b.low(2), b.high(1)), z2[0]), add(cat(b.low(-1), b.high(-2)), z2[1]))
    ops, (term_own, term_partner) = fence((ops, (term_own, term_partner)))
    z3 = b.send(*ops)
    blocks = combine(experts, metas, term_own, term_partner, tokens)

    ops, y2, _ = fence(((add(a.low(1), y1[0]), add(a.high(-1), y1[1])), y2, z2))
    y3 = a.send(*ops)

    ops = (add(b.low(1), z3[0][:h]), add(b.high(-1), z3[1][h:]))
    z4 = b.send(*fence(ops))

    a = Blocks(a.total((y2[1], y2[0]), y3).astype(BF), "z", False)
    u = a.half
    ops = (cat(a.low(4), a.high(3)), cat(a.low(-3), a.high(4)))
    ops, _ = fence((ops, z3))
    z5 = a.send(*ops)

    b = Blocks(b.total((z3[1][:h], z3[0][h:]), z4).astype(BF), "y", False)
    ops = (cat(b.low(2), b.high(1)), cat(b.low(-1), b.high(2)))
    ops, (mine, for_left, for_right, for_far) = fence((ops, blocks))
    y4 = b.send(*ops)
    from_far = shift(for_far, "x", 2)

    ops = (add(cat(a.low(3), a.high(2)), z5[0]), add(cat(a.low(-2), a.high(-3)), z5[1]))
    ops, _ = fence((ops, z4))
    z6 = a.send(*ops)

    y5 = b.send(*fence((add(b.low(1), y4[0][:u]), add(b.high(-1), y4[1][u:]))))
    ops = (add(cat(a.low(2), a.high(1)), z6[0]), add(cat(a.low(-1), a.high(-2)), z6[1]))
    ops, for_left, for_right = fence((ops, for_left, for_right))
    z7 = a.send(*ops)
    from_right, from_left = shift(for_left, "x", -1), shift(for_right, "x", 1)
    z8 = a.send(*fence((add(a.low(1), z7[0][:u]), add(a.high(-1), z7[1][u:]))))
    grad_in = add(mine, from_far, from_right, from_left)
    sum_b = b.total((y4[1][:u], y4[0][u:]), y5)
    sum_a = a.total((z7[1][:u], z7[0][u:]), z8)

    gate_rows, down_rows = width // (ny * nz), ff // (ny * nz)
    lines = gate_rows * ff // 128
    columns = lambda v: v.reshape(-1, gate_rows, 128).transpose(1, 0, 2).reshape(gate_rows, -1)
    out_gate = columns(sum_a[:lines])
    out_up = jnp.concatenate([columns(sum_a[lines:]), columns(sum_b[lines:])], axis=1)
    out_down = sum_b[:lines].reshape(-1, down_rows, 128).transpose(1, 0, 2).reshape(down_rows, width)
    return grad_in, out_gate[None], out_up[None], out_down[None]


def solution(mesh):
    fine = Mesh(mesh.devices.reshape(4, 8, 4, 2), ("y", "z", "x", "core"))
    row = P(("y", "z", "x", "core"), None)
    weight = P(("x", "core"), None, None)
    summed = P(("x", "core"), ("y", "z"), None)
    return jax.shard_map(
        shards,
        mesh=fine,
        in_specs=(row, row, row, row, weight, weight, weight),
        out_specs=(row, summed, summed, summed),
        check_vma=False,
    )
```

```python
import functools

import jax
import jax.numpy as jnp
from jax import lax
from jax.experimental import pallas as pl
from jax.experimental.pallas import tpu as pltpu
from jax.sharding import Mesh
from jax.sharding import PartitionSpec as P

BF = jnp.bfloat16
F32 = jnp.float32
ROWS = (((0,), (0,)), ((), ()))
COLS = (((1,), (1,)), ((), ()))
VMEM_LIMIT = 40 * 1024 * 1024


def shift(value, axis, step):
    n = lax.axis_size(axis)
    return lax.ppermute(value, axis, [(i, (i + step) % n) for i in range(n)])


def add(*terms):
    total = terms[0].astype(F32)
    for term in terms[1:]:
        total = total + term.astype(F32)
    return total.astype(BF)


def params():
    return pltpu.CompilerParams(vmem_limit_bytes=VMEM_LIMIT)


def one_hots(experts_ref, metas):
    own, partner = experts_ref[0].astype(F32), experts_ref[1].astype(F32)
    tables = [m[...].astype(F32) for m in metas]
    hits, gates = [], []
    for table in tables:
        first, second = table[0:1], table[1:2]
        for expert in (own, partner):
            hits.append(jnp.where((first == expert) | (second == expert), 1.0, 0.0))
            gates.append(
                jnp.where(first == expert, table[2:3], 0.0)
                + jnp.where(second == expert, table[3:4], 0.0)
            )
    hit = jnp.concatenate(hits, axis=0)
    tokens = hit.shape[1]
    before = lax.broadcasted_iota(jnp.int32, (tokens, tokens), 0)
    after = lax.broadcasted_iota(jnp.int32, (tokens, tokens), 1)
    upper = jnp.where(before <= after, 1.0, 0.0).astype(BF)
    rank = jnp.dot(hit.astype(BF), upper, preferred_element_type=F32)
    place = jnp.where(hit > 0.0, rank - 1.0, -1.0)
    slots = lax.broadcasted_iota(jnp.int32, (tokens // 2, tokens), 0).astype(F32)
    result = []
    for chip in range(len(tables)):
        halves, scale = [], []
        for k in (2 * chip, 2 * chip + 1):
            half = jnp.where(place[k : k + 1] == slots, 1.0, 0.0)
            halves.append(half)
            scale.append(jnp.sum(half * gates[k], axis=1, keepdims=True))
        result.append((jnp.concatenate(halves, axis=0).astype(BF), jnp.concatenate(scale, axis=0)))
    return result


def fill_tables(experts_ref, metas, table_ref, scale_ref):
    @pl.when(pl.program_id(0) == 0)
    def _():
        for k, (table, scale) in enumerate(one_hots(experts_ref, metas)):
            table_ref[k] = table
            scale_ref[k] = jnp.broadcast_to(scale, scale_ref.shape[1:])


def table_scratch(tokens):
    return [pltpu.VMEM((4, tokens, tokens), BF), pltpu.VMEM((4, tokens, 128), F32)]


def gather_kernel(scaled, experts_ref, *refs):
    metas, (a, b, c, d0, d1), (own_ref, partner_ref) = refs[:4], refs[4:9], refs[9:11]
    table_ref, scale_ref = refs[11:]
    fill_tables(experts_ref, metas, table_ref, scale_ref)
    blocks = [a[...], b[...], c[...], jnp.concatenate([d0[...], d1[...]], axis=0)]
    for k in range(4):
        rows = jnp.dot(table_ref[k], blocks[k], preferred_element_type=F32)
        if scaled:
            rows = scale_ref[k][:, :1] * rows
        rows = rows.astype(BF)
        half = rows.shape[0] // 2
        own_ref[k * half : (k + 1) * half] = rows[:half]
        partner_ref[k * half : (k + 1) * half] = rows[half:]


def meta_specs(tokens):
    return [
        pl.BlockSpec((16, tokens), lambda i: (tokens // 16, 0)),
        pl.BlockSpec((16, tokens), lambda i: (tokens // 16, 0)),
        pl.BlockSpec((16, tokens), lambda i: (tokens // 16, 0)),
        pl.BlockSpec((16, tokens), lambda i: (tokens // 32, 0)),
    ]


def gather_rows(scaled, experts, metas, packets, tokens):
    width = packets[0].shape[1]
    tile = 512
    half = tokens // 2
    heights = (tokens, tokens, tokens, half, half)
    return pl.pallas_call(
        functools.partial(gather_kernel, scaled),
        grid=(width // tile,),
        in_specs=[pl.BlockSpec(memory_space=pltpu.SMEM)]
        + meta_specs(tokens)
        + [pl.BlockSpec((h, tile), lambda i: (0, i)) for h in heights],
        out_specs=[pl.BlockSpec((2 * tokens, tile), lambda i: (0, i))] * 2,
        out_shape=[jax.ShapeDtypeStruct((2 * tokens, width), BF)] * 2,
        scratch_shapes=table_scratch(tokens),
        compiler_params=params(),
        cost_estimate=pl.CostEstimate(
            flops=16 * tokens * tokens * width, bytes_accessed=16 * tokens * width, transcendentals=0
        ),
    )(experts, *metas, *packets)


def combine_kernel(experts_ref, *refs):
    metas, (own, partner), outs = refs[:4], refs[4:6], refs[6:10]
    table_ref, scale_ref = refs[10:]
    fill_tables(experts_ref, metas, table_ref, scale_ref)
    for k in range(4):
        table = table_ref[k]
        half = table.shape[0] // 2
        part = slice(k * half, (k + 1) * half)
        terms = jnp.concatenate([own[part], partner[part]], axis=0)
        outs[k][...] = lax.dot_general(table, terms, ROWS, preferred_element_type=F32).astype(BF)


def combine(experts, metas, own, partner, tokens):
    width = own.shape[1]
    tile = 512
    return pl.pallas_call(
        combine_kernel,
        grid=(width // tile,),
        in_specs=[pl.BlockSpec(memory_space=pltpu.SMEM)]
        + meta_specs(tokens)
        + [pl.BlockSpec((2 * tokens, tile), lambda i: (0, i))] * 2,
        out_specs=[pl.BlockSpec((tokens, tile), lambda i: (0, i))] * 4,
        out_shape=[jax.ShapeDtypeStruct((tokens, width), BF)] * 4,
        scratch_shapes=table_scratch(tokens),
        compiler_params=params(),
        cost_estimate=pl.CostEstimate(
            flops=tokens * width, bytes_accessed=tokens * width, transcendentals=0
        ),
    )(experts, *metas, own, partner)


def forward_kernel(xa, xb, gate_w, up_w, hidden, to_gate, to_up):
    half = xa.shape[0]
    for k, x in enumerate((xa, xb)):
        rows = slice(k * half, (k + 1) * half)
        pre_gate = jnp.dot(x[...], gate_w[0], preferred_element_type=F32)
        pre_up = jnp.dot(x[...], up_w[0], preferred_element_type=F32)
        sigmoid = jax.nn.sigmoid(pre_gate)
        silu = pre_gate * sigmoid
        hidden[rows] = (silu * pre_up).astype(BF)
        to_gate[rows] = pre_up * sigmoid * (1.0 + pre_gate * (1.0 - sigmoid))
        to_up[rows] = silu


def forward(xa, xb, gate_w, up_w):
    half, width = xa.shape
    ff = gate_w.shape[2]
    tile = 256
    whole = pl.BlockSpec((half, width), lambda i: (0, 0))
    weight = pl.BlockSpec((1, width, tile), lambda i: (0, 0, i))
    out = pl.BlockSpec((2 * half, tile), lambda i: (0, i))
    return pl.pallas_call(
        forward_kernel,
        grid=(ff // tile,),
        in_specs=[whole, whole, weight, weight],
        out_specs=[out] * 3,
        out_shape=[
            jax.ShapeDtypeStruct((2 * half, ff), BF),
            jax.ShapeDtypeStruct((2 * half, ff), F32),
            jax.ShapeDtypeStruct((2 * half, ff), F32),
        ],
        compiler_params=params(),
        cost_estimate=pl.CostEstimate(
            flops=8 * half * width * ff, bytes_accessed=4 * width * ff + 24 * half * ff, transcendentals=2 * half * ff
        ),
    )(xa, xb, gate_w, up_w)


def down_kernel(ny, nz, down_rows, gate_rows, me_ref, *refs):
    xa, xb, ga, gb, hidden, to_gate, to_up, down_w, grad_gate, grad_up, part, right, left = refs
    step = pl.program_id(0)
    steps_down = ny // 2
    tile = down_w.shape[1]
    width = xa.shape[1]
    rel = lambda z: lax.rem(z - me_ref[1] + nz, nz)

    @pl.when(step < steps_down)
    def _():
        columns = pl.ds(pl.multiple_of(step * tile, 128), tile)
        grad = jnp.concatenate([ga[...], gb[...]], axis=0)
        grad_hidden = lax.dot_general(grad, down_w[0], COLS, preferred_element_type=F32)
        grad_gate[:, columns] = (grad_hidden * to_gate[...]).astype(BF)
        grad_up[:, columns] = (grad_hidden * to_up[...]).astype(BF)
        block = lax.dot_general(hidden[...], grad, ROWS, preferred_element_type=F32)
        for y in range(2):
            for z in range(nz):
                rows = block[(y * nz + z) * down_rows : (y * nz + z + 1) * down_rows]
                for c in range(width // 256):
                    pair = [rows[:, c * 256 : c * 256 + 128], rows[:, c * 256 + 128 : c * 256 + 256]]
                    pair = jnp.concatenate(pair, axis=0).astype(BF)
                    part[rel(z), 2 * step + y, c * 2 * down_rows : (c + 1) * 2 * down_rows] = pair

    @pl.when(step == steps_down)
    def _():
        half = grad_up.shape[1] // 2
        lines = down_rows * width // 128
        deep = width // ny
        for y in range(ny):
            x = jnp.concatenate(
                [xa[:, y * deep : (y + 1) * deep], xb[:, y * deep : (y + 1) * deep]], axis=0
            )
            block = lax.dot_general(x, grad_up[:, half:], ROWS, preferred_element_type=F32)
            for z in range(nz):
                for c in range(half // 128):
                    rows = block[z * gate_rows : (z + 1) * gate_rows, c * 128 : (c + 1) * 128]
                    at = lines + c * gate_rows
                    part[rel(z), y, at : at + gate_rows] = rows.astype(BF)
        near, far, h = nz // 2 - 1, nz // 2, ny // 2
        right[:h], right[h:] = part[far, :h], part[near, h:]
        left[:h], left[h:] = part[nz - near, :h], part[far, h:]


def down_grads(me, xa, xb, ga, gb, hidden, to_gate, to_up, down_w, ny, nz):
    half, width = xa.shape
    ff = hidden.shape[1]
    down_rows, gate_rows = ff // (ny * nz), width // (ny * nz)
    lines = 3 * gate_rows * ff // 256
    down = ny // 2
    tile = ff // down
    first = lambda i: jnp.minimum(i, down - 1)
    g_spec = pl.BlockSpec((half, width), lambda i, m: (0, 0))
    f_spec = pl.BlockSpec((2 * half, tile), lambda i, m: (0, first(i)))
    grad_spec = pl.BlockSpec((2 * half, ff), lambda i, m: (0, 0))
    sent = pl.BlockSpec((ny, lines, 128), lambda i, m: (0, 0, 0))
    return pl.pallas_call(
        functools.partial(down_kernel, ny, nz, down_rows, gate_rows),
        grid_spec=pltpu.PrefetchScalarGridSpec(
            num_scalar_prefetch=1,
            grid=(down + 1,),
            in_specs=[g_spec] * 4
            + [f_spec] * 3
            + [pl.BlockSpec((1, tile, width), lambda i, m: (0, first(i), 0))],
            out_specs=[
                grad_spec,
                grad_spec,
                pl.BlockSpec((nz, ny, lines, 128), lambda i, m: (0, 0, 0, 0)),
                sent,
                sent,
            ],
        ),
        out_shape=[
            jax.ShapeDtypeStruct((2 * half, ff), BF),
            jax.ShapeDtypeStruct((2 * half, ff), BF),
            jax.ShapeDtypeStruct((nz, ny, lines, 128), BF),
            jax.ShapeDtypeStruct((ny, lines, 128), BF),
            jax.ShapeDtypeStruct((ny, lines, 128), BF),
        ],
        compiler_params=params(),
        cost_estimate=pl.CostEstimate(
            flops=10 * half * width * ff, bytes_accessed=4 * width * ff + 8 * half * width, transcendentals=0
        ),
    )(me, xa, xb, ga, gb, hidden, to_gate, to_up, down_w)


def gate_kernel(nz, gate_rows, me_ref, xa, xb, grad_gate, grad_up, *refs):
    outs, grads = refs[:-1], refs[-1]
    ff = grad_gate.shape[1]

    @pl.when(pl.program_id(0) == 0)
    def _():
        grads[:, :ff] = grad_gate[...]
        grads[:, ff:] = grad_up[:, : ff // 2]

    x = jnp.concatenate([xa[...], xb[...]], axis=0)
    block = lax.dot_general(x, grads[...], ROWS, preferred_element_type=F32)
    each = nz // len(outs)
    for z in range(nz):
        for c in range(grads.shape[1] // 128):
            rows = block[z * gate_rows : (z + 1) * gate_rows, c * 128 : (c + 1) * 128]
            outs[z // each][0, z % each, c * gate_rows : (c + 1) * gate_rows] = rows.astype(BF)


def gate_grads(me, xa, xb, grad_gate, grad_up, ny, nz, far):
    half, width = xa.shape
    ff = grad_gate.shape[1]
    gate_rows = width // (ny * nz)
    lines = 3 * gate_rows * ff // 256
    steps = 1 if far else 3
    turn = lambda i: 2 if far else jnp.where(i == 0, 1, jnp.where(i == 1, 3, 0))
    place = lambda i: 0 if far else jnp.minimum(turn(i), 2)
    x_spec = pl.BlockSpec((half, width // ny), lambda i, m: (0, lax.rem(m[0] + turn(i), ny)))
    grad_spec = pl.BlockSpec((2 * half, ff), lambda i, m: (0, 0))
    outs = 2 if far else 1
    return pl.pallas_call(
        functools.partial(gate_kernel, nz, gate_rows),
        grid_spec=pltpu.PrefetchScalarGridSpec(
            num_scalar_prefetch=1,
            grid=(steps,),
            in_specs=[x_spec, x_spec, grad_spec, grad_spec],
            out_specs=[pl.BlockSpec((1, nz // outs, lines, 128), lambda i, m: (place(i), 0, 0, 0))] * outs,
            scratch_shapes=[pltpu.VMEM((2 * half, ff + ff // 2), BF)],
        ),
        out_shape=[jax.ShapeDtypeStruct((steps, nz // outs, lines, 128), BF)] * outs,
        compiler_params=params(),
        cost_estimate=pl.CostEstimate(
            flops=2 * steps * half * width * ff, bytes_accessed=steps * (half * width + width * ff), transcendentals=0
        ),
    )(me, xa, xb, grad_gate, grad_up)


def terms_kernel(grad_gate, grad_up, gate_w, up_w, first, second):
    half = first.shape[0]
    total = lax.dot_general(grad_gate[...], gate_w[0], COLS, preferred_element_type=F32)
    total = total + lax.dot_general(grad_up[...], up_w[0], COLS, preferred_element_type=F32)
    total = total.astype(BF)
    first[...] = total[:half]
    second[...] = total[half:]


def input_terms(grad_gate, grad_up, gate_w, up_w):
    slots, ff = grad_gate.shape
    width = gate_w.shape[1]
    tile = 512
    grad = pl.BlockSpec((slots, ff), lambda i: (0, 0))
    weight = pl.BlockSpec((1, tile, ff), lambda i: (0, i, 0))
    out = pl.BlockSpec((slots // 2, tile), lambda i: (0, i))
    return pl.pallas_call(
        terms_kernel,
        grid=(width // tile,),
        in_specs=[grad, grad, weight, weight],
        out_specs=[out, out],
        out_shape=[jax.ShapeDtypeStruct((slots // 2, width), BF)] * 2,
        compiler_params=params(),
        cost_estimate=pl.CostEstimate(
            flops=slots * ff, bytes_accessed=slots * ff, transcendentals=0
        ),
    )(grad_gate, grad_up, gate_w, up_w)


def cat(first, second):
    return jnp.concatenate([first, second], axis=0)


class Blocks:
    def __init__(self, value, axis, counted_from_here):
        self.value, self.axis, self.n = value, axis, lax.axis_size(axis)
        self.half = value.shape[1] // 2
        self.start = 0 if counted_from_here else lax.axis_index(axis)

    def block(self, k):
        if self.value.shape[0] == self.n - 1:
            return self.value[min(k % self.n, self.n - 2)]
        return lax.dynamic_index_in_dim(self.value, (self.start + k + self.n) % self.n, 0, keepdims=False)

    def low(self, k):
        return self.block(k)[: self.half]

    def high(self, k):
        return self.block(k)[self.half :]

    def send(self, right, left):
        return shift(right, self.axis, 1), shift(left, self.axis, -1)

    def total(self, *pairs):
        result = self.block(0).astype(F32)
        for low, high in pairs:
            result = result + cat(low, high).astype(F32)
        return result


def shards(inputs, grad_out, expert_ids, gate_probs, w_gate, w_up, w_down):
    tokens, width = inputs.shape
    ff = w_gate.shape[2]
    ny, nz = lax.axis_size("y"), lax.axis_size("z")
    half = tokens // 2
    chip, core = lax.axis_index("x"), lax.axis_index("core")
    experts = jnp.stack([2 * chip + core, 2 * chip + 1 - core]).astype(jnp.int32)
    me = jnp.stack([lax.axis_index("y"), lax.axis_index("z")]).astype(jnp.int32)
    fence = lax.optimization_barrier

    table = jnp.concatenate([expert_ids.T.astype(BF), gate_probs.T], axis=0)
    table = jnp.pad(table, ((0, 12), (0, width - tokens)))
    packet = jnp.concatenate([inputs, table], axis=0)

    x_left, x_right = shift(packet, "x", 1), shift(packet, "x", -1)
    g_left, g_right = shift(grad_out, "x", 1), shift(grad_out, "x", -1)
    x_low, x_high = shift(x_left[:half], "x", 1), shift(x_right[half:], "x", -1)
    g_low, g_high = shift(g_left[:half], "x", 1), shift(g_right[half:], "x", -1)
    metas = (packet, x_left, x_right, x_high)

    xa, x_partner = gather_rows(False, experts, metas, (packet, x_left, x_right, x_low, x_high), tokens)
    xb = shift(x_partner, "core", 1)
    hidden, to_gate, to_up = forward(xa, xb, w_gate, w_up)
    ga, g_partner = gather_rows(True, experts, metas, (grad_out, g_left, g_right, g_low, g_high), tokens)
    gb = shift(g_partner, "core", 1)
    grad_gate, grad_up, part_b, b_right, b_left = down_grads(
        me, xa, xb, ga, gb, hidden, to_gate, to_up, w_down, ny, nz
    )

    b = Blocks(part_b, "z", True)
    h = b.half
    a_low, a_high = gate_grads(me, xa, xb, grad_gate, grad_up, ny, nz, True)
    b_right, b_left, a_low, a_high, grads = fence((b_right, b_left, a_low[0], a_high[0], (grad_gate, grad_up)))
    z1 = b.send(b_right, b_left)
    y1 = shift(a_low, "y", 1), shift(a_high, "y", -1)
    (part_a,) = gate_grads(me, xa, xb, *grads, ny, nz, False)
    terms = input_terms(*grads, w_gate, w_up)

    ops = (add(cat(b.low(3), b.high(2)), z1[0]), add(cat(b.low(-2), b.high(-3)), z1[1]))
    ops, (term_own, term_other), part_a = fence((ops, terms, part_a))
    a = Blocks(part_a, "y", True)
    z2 = b.send(*ops)
    term_partner = shift(term_other, "core", 1)

    ops, y1, _ = fence(((a.high(1), a.low(-1)), y1, z1))
    y2 = a.send(*ops)

    ops = (add(cat(b.low(2), b.high(1)), z2[0]), add(cat(b.low(-1), b.high(-2)), z2[1]))
    ops, (term_own, term_partner) = fence((ops, (term_own, term_partner)))
    z3 = b.send(*ops)
    blocks = combine(experts, metas, term_own, term_partner, tokens)

    ops, y2, _ = fence(((add(a.low(1), y1[0]), add(a.high(-1), y1[1])), y2, z2))
    y3 = a.send(*ops)

    ops = (add(b.low(1), z3[0][:h]), add(b.high(-1), z3[1][h:]))
    z4 = b.send(*fence(ops))

    a = Blocks(a.total((y2[1], y2[0]), y3).astype(BF), "z", False)
    u = a.half
    ops = (cat(a.low(4), a.high(3)), cat(a.low(-3), a.high(4)))
    ops, _ = fence((ops, z3))
    z5 = a.send(*ops)

    b = Blocks(b.total((z3[1][:h], z3[0][h:]), z4).astype(BF), "y", False)
    ops = (cat(b.low(2), b.high(1)), cat(b.low(-1), b.high(2)))
    ops, (mine, for_left, for_right, for_far) = fence((ops, blocks))
    y4 = b.send(*ops)
    from_far = shift(for_far, "x", 2)

    ops = (add(cat(a.low(3), a.high(2)), z5[0]), add(cat(a.low(-2), a.high(-3)), z5[1]))
    ops, _ = fence((ops, z4))
    z6 = a.send(*ops)

    y5 = b.send(*fence((add(b.low(1), y4[0][:u]), add(b.high(-1), y4[1][u:]))))
    ops = (add(cat(a.low(2), a.high(1)), z6[0]), add(cat(a.low(-1), a.high(-2)), z6[1]))
    ops, for_left, for_right = fence((ops, for_left, for_right))
    z7 = a.send(*ops)
    from_right, from_left = shift(for_left, "x", -1), shift(for_right, "x", 1)
    z8 = a.send(*fence((add(a.low(1), z7[0][:u]), add(a.high(-1), z7[1][u:]))))
    grad_in = add(mine, from_far, from_right, from_left)
    sum_b = b.total((y4[1][:u], y4[0][u:]), y5)
    sum_a = a.total((z7[1][:u], z7[0][u:]), z8)

    gate_rows, down_rows = width // (ny * nz), ff // (ny * nz)
    lines = gate_rows * ff // 128
    columns = lambda v: v.reshape(-1, gate_rows, 128).transpose(1, 0, 2).reshape(gate_rows, -1)
    out_gate = columns(sum_a[:lines])
    out_up = jnp.concatenate([columns(sum_a[lines:]), columns(sum_b[lines:])], axis=1)
    out_down = sum_b[:lines].reshape(-1, down_rows, 128).transpose(1, 0, 2).reshape(down_rows, width)
    return grad_in, out_gate[None], out_up[None], out_down[None]


def solution(mesh):
    fine = Mesh(mesh.devices.reshape(4, 8, 4, 2), ("y", "z", "x", "core"))
    row = P(("y", "z", "x", "core"), None)
    weight = P(("x", "core"), None, None)
    summed = P(("x", "core"), ("y", "z"), None)
    return jax.shard_map(
        shards,
        mesh=fine,
        in_specs=(row, row, row, row, weight, weight, weight),
        out_specs=(row, summed, summed, summed),
        check_vma=False,
    )
```
